128 devices in a mesh: wide: 16 (over z, x), narrow: 8 (over y, core).
Axes of the slice: x: 4, y: 4, z: 4, core: 2. Of those that a mesh axis runs over, the one named last changes fastest.
Arguments:
- node_latent: float32 [32768, 512], P(('wide', 'narrow')), may hold values from -6 to 6
- edge_latent: float32 [131072, 512], P(('wide', 'narrow')), may hold values from -6 to 6
- edge_slot: int32 [131072], P(('wide', 'narrow')), may hold values from 0 to 1279, as said below
- edge_receiver: int32 [131072], P(('wide', 'narrow')), may hold values from 0 to 255
- send_rows: int32 [128, 128, 8], P(('wide', 'narrow')), may hold values from 0 to 255
- node_cotangent: float32 [32768, 512], P(('wide', 'narrow')), may hold values from -6 to 6
- edge_cotangent: float32 [131072, 512], P(('wide', 'narrow')), may hold values from -6 to 6
- edge_w1: float32 [1536, 512], replicated, may hold values from -0.15625 to 0.15625
- edge_b1: float32 [512], replicated, may hold values from -3 to 3
- edge_w2: float32 [512, 512], replicated, may hold values from -0.25 to 0.25
- edge_gain: float32 [512], replicated, may hold values from 0.1 to 1.9
- node_w1: float32 [1024, 512], replicated, may hold values from -0.1875 to 0.1875
- node_b1: float32 [512], replicated, may hold values from -3 to 3
- node_w2: float32 [512, 512], replicated, may hold values from -0.25 to 0.25
- node_gain: float32 [512], replicated, may hold values from 0.1 to 1.9
Outputs:
- new_nodes: float32 [32768, 512], P(('wide', 'narrow'))
- node_grad: float32 [32768, 512], P(('wide', 'narrow'))
- edge_grad: float32 [131072, 512], P(('wide', 'narrow'))
- edge_w1_grad: float32 [1536, 512], replicated
- edge_b1_grad: float32 [512], replicated
- edge_w2_grad: float32 [512, 512], replicated
- edge_gain_grad: float32 [512], replicated
- node_w1_grad: float32 [1024, 512], replicated
- node_b1_grad: float32 [512], replicated
- node_w2_grad: float32 [512, 512], replicated
- node_gain_grad: float32 [512], replicated
The draws below stay inside these ranges and needn't reach their ends.
Inputs may be any that keep to these rules, and one draw needn't show every extreme that they name: `edge_slot`: of the 8 slots that one device sends to another, the edges of the receiving device read only the first k, k from 1 to 8 for each pair of devices; every device reads the last of the 8 slots of at least one other device. Slots that no edge reads still hold node indices.
All inputs are finite; a program needn't handle non-finite values.
Results may differ from the reference program's by a relative error of at most 0.000086.
Values sent between devices are 32-bit elements; how exact they have to be, the bound alone decides.
A program may use at most 128 MiB of HBM per device.

```python
import jax
import jax.numpy as jnp
from jax import lax

LAT = 512
NODE_DEV = 256
EDGE_DEV = 1024
CAP = 8
NODES = 32768
EDGES = 131072
N_WIDE = 16
N_NARROW = 8


def draw_edge_slot(key, part):
    key = jax.random.fold_in(key, 7)
    keys = jax.random.split(key, 5)
    devices = N_WIDE * N_NARROW
    peer_count = jax.random.randint(keys[0], (devices, devices), 1, CAP + 1)
    source = jnp.arange(devices, dtype=jnp.int32)[:, None]
    target = jnp.arange(devices, dtype=jnp.int32)[None, :]
    peer_count = jnp.where(target == (source + 1) % devices, CAP, peer_count)
    owner = jnp.broadcast_to(jnp.arange(devices, dtype=jnp.int32)[:, None], (devices, EDGE_DEV))
    local = jax.random.randint(keys[1], (devices, EDGE_DEV), 0, NODE_DEV)
    peer = jax.random.randint(keys[2], (devices, EDGE_DEV), 0, devices)
    column = jax.random.randint(keys[3], (devices, EDGE_DEV), 0, CAP) % peer_count[peer, owner]
    remote = NODE_DEV + peer * CAP + column
    pick = jax.random.randint(keys[4], (devices, EDGE_DEV), 0, 2)
    slot = jnp.where(pick == 0, local, remote)
    position = jnp.arange(EDGE_DEV, dtype=jnp.int32)[None, :]
    last = NODE_DEV + (owner + devices - 1) % devices * CAP + CAP - 1
    slot = jnp.where(position == EDGE_DEV - 1, last, slot)
    slot = jnp.where(position == 0, 0, slot)
    return slot.reshape(-1).astype(jnp.int32)


def place_ends(drawn, key, smallest, high):
    longest = drawn.shape.index(max(drawn.shape))
    spots = []
    for shift in (0, 1):
        where = [jax.random.randint(jax.random.fold_in(key, axis), (), 0, length) for axis, length in enumerate(drawn.shape)]
        where[longest] = (where[longest] + shift) % drawn.shape[longest]
        spots.append(tuple(where))
    return drawn.at[spots[0]].set(smallest).at[spots[1]].set(high)


def shard_levels(stream_key, shape, pieces, low, top_value):
    loudness, own = 1.0, jax.random.fold_in(stream_key, 6)
    for dim, blocks in pieces:
        steps = jnp.exp(jax.random.uniform(jax.random.fold_in(own, dim), (blocks,), jnp.float32, low / len(pieces), top_value / len(pieces)))
        loudness = loudness * jnp.repeat(steps, shape[dim] // blocks).reshape([-1 if axis == dim else 1 for axis in range(len(shape))])
    return loudness


def bell_draw(key, extent, width, most, cuts=(), kind=jnp.bfloat16):
    loudness = shard_levels(key, extent, cuts, -0.22, 0.18) if cuts else 1.0
    result = jax.random.normal(key, extent, jnp.float32) * width * loudness
    return jnp.minimum(jnp.maximum(result, -most), most).astype(kind)


def setup_inputs(seed: int = 0) -> dict:
    arg_keys = jax.random.split(jax.random.key(seed), 16)
    return {
        "node_latent": bell_draw(arg_keys[0], (NODES, LAT), 1.0, 6.0, ((0, 128),), jnp.float32),
        "edge_latent": bell_draw(arg_keys[1], (EDGES, LAT), 1.0, 6.0, ((0, 128),), jnp.float32),
        "edge_slot": draw_edge_slot(jax.random.fold_in(arg_keys[15], 71), 0),
        "edge_receiver": place_ends(jax.random.randint(arg_keys[3], (EDGES,), 0, NODE_DEV), jax.random.fold_in(arg_keys[3], 1), 0, NODE_DEV - 1).astype(jnp.int32),
        "send_rows": place_ends(jax.random.randint(arg_keys[4], (N_WIDE * N_NARROW, N_WIDE * N_NARROW, CAP), 0, NODE_DEV), jax.random.fold_in(arg_keys[4], 1), 0, NODE_DEV - 1).astype(jnp.int32),
        "node_cotangent": bell_draw(arg_keys[5], (NODES, LAT), 1.0, 6.0, ((0, 128),), jnp.float32),
        "edge_cotangent": bell_draw(arg_keys[6], (EDGES, LAT), 1.0, 6.0, ((0, 128),), jnp.float32),
        "edge_w1": bell_draw(arg_keys[7], (3 * LAT, LAT), (3 * LAT) ** -0.5, 0.15625, (), jnp.float32),
        "edge_b1": bell_draw(arg_keys[8], (LAT,), 0.5, 3.0, (), jnp.float32),
        "edge_w2": bell_draw(arg_keys[9], (LAT, LAT), LAT ** -0.5, 0.25, (), jnp.float32),
        "edge_gain": jnp.clip(1.0 + 0.18 * jax.random.normal(arg_keys[10], (LAT,), jnp.float32), 0.1, 1.9),
        "node_w1": bell_draw(arg_keys[11], (2 * LAT, LAT), (2 * LAT) ** -0.5, 0.1875, (), jnp.float32),
        "node_b1": bell_draw(arg_keys[12], (LAT,), 0.5, 3.0, (), jnp.float32),
        "node_w2": bell_draw(arg_keys[13], (LAT, LAT), LAT ** -0.5, 0.25, (), jnp.float32),
        "node_gain": jnp.clip(1.0 + 0.18 * jax.random.normal(arg_keys[14], (LAT,), jnp.float32), 0.1, 1.9),
    }


highest = lax.Precision.HIGHEST

def layer_norm(values, gain):
    centre = values - lax.optimization_barrier(jnp.mean(values, axis=-1, keepdims=True))
    spread = lax.optimization_barrier(jnp.mean(centre * centre, axis=-1, keepdims=True))
    return centre * lax.rsqrt(spread + 1e-05) * gain

def edge_update(edge_latent, sender_rows, receiver_rows, edge_w1, edge_b1, edge_w2, edge_gain):
    joined = jnp.concatenate([edge_latent, sender_rows, receiver_rows], axis=1)
    hidden = jax.nn.silu(jnp.dot(joined, edge_w1, precision=highest, preferred_element_type=jnp.float32) + edge_b1)
    return layer_norm(jnp.dot(hidden, edge_w2, precision=highest, preferred_element_type=jnp.float32), edge_gain)

def node_update(node_latent, aggregate, node_w1, node_b1, node_w2, node_gain):
    joined = jnp.concatenate([node_latent, aggregate], axis=1)
    hidden = jax.nn.silu(jnp.dot(joined, node_w1, precision=highest, preferred_element_type=jnp.float32) + node_b1)
    return layer_norm(jnp.dot(hidden, node_w2, precision=highest, preferred_element_type=jnp.float32), node_gain)

def reference(node_latent, edge_latent, edge_slot, edge_receiver, send_rows, node_cotangent, edge_cotangent, edge_w1, edge_b1, edge_w2, edge_gain, node_w1, node_b1, node_w2, node_gain):
    owner = (jnp.arange(EDGES, dtype=jnp.int32) // EDGE_DEV).astype(jnp.int32)
    remote = jnp.maximum(edge_slot - NODE_DEV, 0).astype(jnp.int32)
    peer = (remote // CAP).astype(jnp.int32)
    column = (remote % CAP).astype(jnp.int32)
    far_row = send_rows[peer, owner, column]
    sender = jnp.where(edge_slot < NODE_DEV, owner * NODE_DEV + edge_slot, peer * NODE_DEV + far_row).astype(jnp.int32)
    receiver = (owner * NODE_DEV + edge_receiver).astype(jnp.int32)

    def forward(nodes_in, edges_in, ew1, eb1, ew2, egain, nw1, nb1, nw2, ngain):
        message = edge_update(edges_in, nodes_in[sender], nodes_in[receiver], ew1, eb1, ew2, egain)
        aggregate = jax.ops.segment_sum(message, receiver, num_segments=NODES)
        updated = nodes_in + node_update(nodes_in, aggregate, nw1, nb1, nw2, ngain)
        return (updated, edges_in + message)
    outputs, pull = jax.vjp(forward, node_latent, edge_latent, edge_w1, edge_b1, edge_w2, edge_gain, node_w1, node_b1, node_w2, node_gain)
    grads = pull((node_cotangent, edge_cotangent))
    return (outputs[0], grads[0], grads[1], grads[2], grads[3], grads[4], grads[5], grads[6], grads[7], grads[8], grads[9])
```

```python
import functools

import jax
import jax.numpy as jnp
from jax import lax
from jax.experimental import pallas as pl
from jax.experimental.pallas import tpu as pltpu
from jax.sharding import PartitionSpec as P

MESH = pl.DeviceIdType.MESH
F32, BF16, I32 = jnp.float32, jnp.bfloat16, jnp.int32
W = 512
NODES = 256
EDGES = 1024
SLOTS = 1280
CH = 256

FLAT = 15360
ROT = 5120
SIZE = (640, 160, 40)
HALF = (320, 80, 24)
ORDERS = ((0, 1, 2), (1, 2, 0), (2, 0, 1))
SEMS = 35
UNITS = {"nw1a": 0, "nw1b": 4, "nw2": 8, "w2": 12, "w1c": 16, "w1a": 20, "w1b": 24, "small": 28}
WROW = {"w1a": 0, "w1b": 512, "w1c": 1024, "w2": 1536, "nw1a": 2048, "nw1b": 2560, "nw2": 3072}


def coords():
    w = lax.axis_index("wide")
    n = lax.axis_index("narrow")
    return w % 4, n // 2, w // 4, n % 2


def device(x, y, z, c):
    return (z * 4 + x, y * 2 + c)


def wait(ref, sem):
    pltpu.make_async_copy(ref, ref, sem).wait()


def rows(start, n):
    return pl.ds(pl.multiple_of(start, 8), n)


def split(v):
    high = v.astype(BF16)
    return high, (v - high.astype(F32)).astype(BF16)


def dot(a, b):
    return jnp.dot(a, b, preferred_element_type=F32)


def dot_nt(a, b):
    return lax.dot_general(a, b, (((1,), (1,)), ((), ())), preferred_element_type=F32)


def dot_tn(a, b):
    return lax.dot_general(a, b, (((0,), (0,)), ((), ())), preferred_element_type=F32)


def three(op, a, b):
    return op(a[0], b[0]) + op(a[1], b[0]) + op(a[0], b[1])


def two(one_hot, pair):
    return dot(one_hot, pair[0]) + dot(one_hot, pair[1])


def reduce_rotation(rot, buf, out, halves_in, send, recv, started):
    here = coords()
    core = here[3]
    order = ORDERS[rot]
    pos = [here[a] for a in order]

    def shifted(stage, by):
        c = list(here)
        c[order[stage]] = (c[order[stage]] + by) % 4
        return device(*c)

    sibling = device(here[0], here[1], here[2], 1 - core)

    def post(src, dst, k, to):
        d = pltpu.make_async_remote_copy(
            src_ref=src,
            dst_ref=dst,
            send_sem=send.at[rot, k],
            recv_sem=recv.at[rot, k],
            device_id=to,
            device_id_type=MESH,
        )
        d.start()
        started.append(d)

    base = rot * ROT
    mine = base + core * 2560
    other = base + (1 - core) * 2560
    post(buf.at[rows(other, 2560)], out.at[rows(other, 2560)], 0, sibling)
    yield
    wait(out.at[rows(mine, 2560)], recv.at[rot, 0])

    def add(i, _):
        r = rows(mine + i * 320, 320)
        buf[r] = buf[r] + out[r]
        return 0

    lax.fori_loop(0, 8, add, 0)
    region = mine
    into = 0
    for s in range(3):
        L = SIZE[s]
        A = HALF[s]
        B = L - A
        j = pos[s]
        k = 1 + 6 * s
        at = lambda q, region=region, j=j, L=L: region + ((j + q) % 4) * L
        first_a, first_b = rows(into, A), rows(into + A, B)
        plus_a, plus_b = rows(into + L, A), rows(into + L + A, B)
        minus_a, minus_b = rows(into + 2 * L, A), rows(into + 2 * L + A, B)
        land = lambda r: halves_in.at[rot, r]
        up, down = shifted(s, 1), shifted(s, -1)
        post(buf.at[rows(at(2), A)], land(first_a), k, down)
        post(buf.at[rows(at(2) + A, B)], land(first_b), k + 1, up)
        post(buf.at[rows(at(-1) + A, B)], land(plus_b), k + 2, down)
        post(buf.at[rows(at(1), A)], land(minus_a), k + 3, up)
        yield
        wait(land(first_a), recv.at[rot, k])
        r = rows(at(-1), A)
        buf[r] = buf[r] + halves_in[rot, first_a]
        post(buf.at[r], land(plus_a), k + 4, down)
        wait(land(first_b), recv.at[rot, k + 1])
        r = rows(at(1) + A, B)
        buf[r] = buf[r] + halves_in[rot, first_b]
        post(buf.at[r], land(minus_b), k + 5, up)
        yield
        wait(land(plus_b), recv.at[rot, k + 2])
        wait(land(minus_a), recv.at[rot, k + 3])
        wait(land(plus_a), recv.at[rot, k + 4])
        wait(land(minus_b), recv.at[rot, k + 5])
        r = rows(at(0), L)
        total = buf[r] + halves_in[rot, rows(into + L, L)] + halves_in[rot, rows(into + 2 * L, L)]
        if s < 2:
            buf[r] = total
        else:
            out[r] = total
        region = region + j * L
        into += 3 * L
    for s in (2, 1, 0):
        L = SIZE[s]
        A = HALF[s]
        B = L - A
        j = pos[s]
        k = 19 + 4 * s
        region = region - j * L
        at = lambda q, region=region, j=j, L=L: region + ((j + q) % 4) * L
        up, down = shifted(s, 1), shifted(s, -1)
        own = out.at[rows(at(0), L)]
        post(own, own, k, up)
        post(own, own, k + 1, down)
        if s == 0:
            post(own, own, 31, sibling)
        yield
        left, right = out.at[rows(at(-1), L)], out.at[rows(at(1), L)]
        wait(left, recv.at[rot, k])
        part = out.at[rows(at(-1), A)]
        post(part, part, k + 2, up)
        if s == 0:
            post(left, left, 32, sibling)
        wait(right, recv.at[rot, k + 1])
        part = out.at[rows(at(1) + A, B)]
        post(part, part, k + 3, down)
        if s == 0:
            post(right, right, 33, sibling)
        yield
        wait(out.at[rows(at(2), A)], recv.at[rot, k + 2])
        wait(out.at[rows(at(2) + A, B)], recv.at[rot, k + 3])
    opposite = out.at[rows(at(2), L)]
    post(opposite, opposite, 34, sibling)
    yield
    for n in range(4):
        wait(out.at[rows(other, 640)], recv.at[rot, 31 + n])


def kernel(
    slot_ref, receiver_ref, list_ref, vector_ref,
    node_h, edge_h, ncot_h, ecot_h, w1_h, w2_h, nw1_h, nw2_h,
    new_nodes_h, node_grad_h, edge_grad_h, w1g_h, w2g_h, nw1g_h, nw2g_h, small_h,
    node_v, node_hi, node_lo, ncot, ecot, pre, whi, wlo, sbuf, rbuf, abuf,
    oslot, orecv, orecv_t, osend, osend_t, tabh, tabl, sh, sl, hh, hl, dph, dpl,
    rstd_v, agg, npre, carry, gloc, rsum, buf, out, halves_in,
    lsem, send1, recv1, send2, recv2, send, recv,
):
    x, y, z, c = coords()
    me = (z * 4 + x) * 8 + y * 2 + c

    def peer(d):
        return (z + d // 32) % 4 * 4 + (x + d // 8) % 4, (y + d // 2) % 4 * 2 + (c + d) % 2

    def load(src, dst, k):
        d = pltpu.make_async_copy(src, dst, lsem.at[k])
        d.start()
        return d

    xhat = rbuf
    load_node = load(node_h, node_v, 0)
    load_edge = load(edge_h, pre, 1)
    load_ncot = load(ncot_h, ncot, 2)
    blocks = [(w1_h, 0), (w1_h, 512), (w1_h, 1024), (w2_h, 0), (nw1_h, 0), (nw1_h, 512), (nw2_h, 0)]

    def load_weights(b):
        src, at = blocks[b]
        return load(src.at[pl.ds(at, 512)], ecot.at[pl.ds(b % 2 * 512, 512)], 3 + b)

    loading = {b: load_weights(b) for b in (0, 1)}
    barrier = pltpu.get_barrier_semaphore()

    def greet(i, _):
        pl.semaphore_signal(barrier, inc=1, device_id=peer(i), device_id_type=MESH)
        return 0

    lax.fori_loop(1, 128, greet, 0)

    def line(ref, i):
        return jnp.broadcast_to(ref[pl.ds(i, 1), :], (128, 128))

    def across(i, ref, store, n):
        lanes = lax.broadcasted_iota(I32, (128, 128), 1)
        column = line(ref, i).T
        for q in range(n // 128):
            store[rows(i * 128, 128), q * 128 : q * 128 + 128] = jnp.where(
                column == lanes + q * 128, 1.0, 0.0
            ).astype(BF16)

    def hot(i, _):
        across(i, list_ref, osend, NODES)
        return 0

    lax.fori_loop(0, 8, hot, 0)
    load_node.wait()
    nhi, nlo = split(node_v[...])
    node_hi[...] = nhi
    node_lo[...] = nlo

    def gather(i, _):
        r = rows(i * CH, CH)
        sbuf[r] = two(osend[r], (node_hi[...], node_lo[...]))
        return 0

    lax.fori_loop(0, EDGES // CH, gather, 0)
    mine8 = rows(me * 8, 8)
    rbuf[mine8] = sbuf[mine8]
    pl.semaphore_wait(barrier, 127)

    def send_rows(i, _):
        w, n = peer(i * 37 % 128)
        pltpu.make_async_remote_copy(
            src_ref=sbuf.at[rows((w * 8 + n) * 8, 8)],
            dst_ref=rbuf.at[mine8],
            send_sem=send1,
            recv_sem=recv1,
            device_id=(w, n),
            device_id_type=MESH,
        ).start()
        return 0

    lax.fori_loop(1, 128, send_rows, 0)

    for b in range(7):
        loading[b].wait()

        def cut(i, _, b=b):
            hi, lo = split(ecot[rows(b % 2 * 512 + i * 128, 128)])
            whi[rows(b * 512 + i * 128, 128)] = hi
            wlo[rows(b * 512 + i * 128, 128)] = lo
            return 0

        lax.fori_loop(0, 4, cut, 0)
        if b + 2 < 7:
            loading[b + 2] = load_weights(b + 2)
    load_ecot = load(ecot_h, ecot, 10)

    def weight(name):
        r = pl.ds(WROW[name], 512)
        return whi[r], wlo[r]

    def hot_edges(i, _):
        across(i, slot_ref, oslot, SLOTS)
        across(i, receiver_ref, orecv, NODES)
        return 0

    lax.fori_loop(0, 8, hot_edges, 0)

    def down(ref, i, first, n):
        return jnp.where(
            jnp.broadcast_to(ref[pl.ds(i, 1), :], (n, 128))
            == lax.broadcasted_iota(I32, (n, 128), 0) + first,
            1.0,
            0.0,
        ).astype(BF16)

    for i in range(8):
        lanes = slice(i % 2 * 128, i % 2 * 128 + 128)
        orecv_t[i // 2, :, lanes] = down(receiver_ref, i, 0, NODES)
        osend_t[i // 2, :, lanes] = down(list_ref, i, 0, NODES)

    node_pair = lambda: (node_hi[...], node_lo[...])
    projected = split(three(dot, node_pair(), weight("w1c")))
    agg[...] = projected[0].astype(F32)
    gloc[...] = projected[1].astype(F32)
    npre[...] = three(dot, node_pair(), weight("nw1a")) + vector_ref[2:3, :]
    load_edge.wait()

    def first_layer(i, _):
        r = rows(i * CH, CH)
        pair = split(pre[r])
        pre[r] = (
            three(dot, pair, weight("w1a"))
            + two(orecv[r], (agg[...].astype(BF16), gloc[...].astype(BF16)))
            + vector_ref[0:1, :]
        )
        return 0

    lax.fori_loop(0, EDGES // CH, first_layer, 0)
    tabh[0:NODES] = node_hi[...]
    tabl[0:NODES] = node_lo[...]
    agg[...] = jnp.zeros_like(agg)

    wait(rbuf.at[pl.ds(0, 1016)], recv1)
    wait(sbuf.at[pl.ds(0, 1016)], send1)

    def cut_table(i, _):
        hi, lo = split(rbuf[rows(i * 256, 256)])
        tabh[rows(256 + i * 256, 256)] = hi
        tabl[rows(256 + i * 256, 256)] = lo
        return 0

    lax.fori_loop(0, 4, cut_table, 0)

    def forward(i, _):
        r = rows(i * CH, CH)
        hot = oslot[r, 0:SLOTS]
        senders = dot(hot, tabh[...]).astype(BF16), dot(hot, tabl[...]).astype(BF16)
        sh[r] = senders[0]
        sl[r] = senders[1]
        v = pre[r] + three(dot, senders, weight("w1b"))
        s = 1.0 / (1.0 + jnp.exp(-v))
        pre[r] = s * (1.0 + v * (1.0 - s))
        hidden = split(v * s)
        hh[r] = hidden[0]
        hl[r] = hidden[1]
        zed = three(dot, hidden, weight("w2"))
        centre = zed - jnp.mean(zed, axis=1, keepdims=True)
        rstd = lax.rsqrt(jnp.mean(centre * centre, axis=1, keepdims=True) + 1e-05)
        scaled = centre * rstd
        xhat[r] = scaled
        rstd_v[r] = jnp.broadcast_to(rstd, (CH, 128))
        agg[...] += two(orecv_t[i], split(scaled))
        return 0

    lax.fori_loop(0, EDGES // CH, forward, 0)

    aggregate = split(agg[...] * vector_ref[1:2, :])
    v = npre[...] + three(dot, aggregate, weight("nw1b"))
    s = 1.0 / (1.0 + jnp.exp(-v))
    slope = s * (1.0 + v * (1.0 - s))
    hidden = split(v * s)
    zed = three(dot, hidden, weight("nw2"))
    centre = zed - jnp.mean(zed, axis=1, keepdims=True)
    rstd = lax.rsqrt(jnp.mean(centre * centre, axis=1, keepdims=True) + 1e-05)
    scaled = centre * rstd
    npre[...] = node_v[...] + scaled * vector_ref[3:4, :]
    store_nodes = load(npre, new_nodes_h, 11)
    load_ncot.wait()
    ngain_grad = jnp.sum(ncot[...] * scaled, axis=0, keepdims=True)
    cot = ncot[...] * vector_ref[3:4, :]
    dz = split(
        rstd
        * (
            cot
            - jnp.mean(cot, axis=1, keepdims=True)
            - scaled * jnp.mean(cot * scaled, axis=1, keepdims=True)
        )
    )
    dpre = three(dot_nt, dz, weight("nw2")) * slope
    nb1_grad = jnp.sum(dpre, axis=0, keepdims=True)
    dpre = split(dpre)
    dagg = split(three(dot_nt, dpre, weight("nw1b")))
    ncot[...] += three(dot_nt, dpre, weight("nw1a"))

    def put(unit, value, first=0):
        for q in range(4):
            buf[rows((unit + q) * 512 + first, value.shape[0])] = value[:, q * 128 : q * 128 + 128]

    put(UNITS["nw2"], three(dot_tn, hidden, dz))
    put(UNITS["nw1a"], three(dot_tn, node_pair(), dpre))
    put(UNITS["nw1b"], three(dot_tn, aggregate, dpre))
    started = []
    rotations = [
        reduce_rotation(r, buf, out, halves_in, send, recv, started) for r in range(3)
    ]
    next(rotations[0])

    load_ecot.wait()
    carry[...] = jnp.zeros_like(carry)
    agg[...] = dagg[0].astype(F32)
    gloc[...] = dagg[1].astype(F32)

    def backward(i, _):
        r = rows(i * CH, CH)
        scaled = xhat[r]
        mcot = ecot[r] + two(orecv[r], (agg[...].astype(BF16), gloc[...].astype(BF16)))
        carry[0:1] += jnp.sum(mcot * scaled, axis=0, keepdims=True)
        cot = mcot * vector_ref[1:2, :]
        dz = split(
            rstd_v[r][:, 0:1]
            * (
                cot
                - jnp.mean(cot, axis=1, keepdims=True)
                - scaled * jnp.mean(cot * scaled, axis=1, keepdims=True)
            )
        )
        tabh[r] = dz[0]
        tabl[r] = dz[1]
        dpre = three(dot_nt, dz, weight("w2")) * pre[r]
        carry[1:2] += jnp.sum(dpre, axis=0, keepdims=True)
        dpre = split(dpre)
        dph[r] = dpre[0]
        dpl[r] = dpre[1]
        return 0

    lax.fori_loop(0, EDGES // CH, backward, 0)
    next(rotations[0])
    load_edge = load(edge_h, pre, 12)

    def scatter(first):
        for i in range(8):
            oslot[0:256, i * 128 : i * 128 + 128] = down(slot_ref, i, first, 256)
        return two(oslot[0:256, 0:EDGES], (dph[...], dpl[...]))

    def plane(n, _):
        dz_ = (n + 1) % 4
        at = (z + dz_) % 4 * 256
        sbuf[rows(at, 256)] = scatter(NODES + at)

        def give(i, _):
            w, nn = peer(dz_ * 32 + i * 13 % 32)
            pltpu.make_async_remote_copy(
                src_ref=sbuf.at[rows((w * 8 + nn) * 8, 8)],
                dst_ref=abuf.at[mine8],
                send_sem=send2,
                recv_sem=recv2,
                device_id=(w, nn),
                device_id_type=MESH,
            ).start()
            return 0

        lax.fori_loop(jnp.where(dz_ == 0, 1, 0), 32, give, 0)
        return 0

    lax.fori_loop(0, 4, plane, 0)
    next(rotations[0])
    abuf[mine8] = sbuf[mine8]
    gloc[...] = scatter(0)
    rsum[...] = sum(
        two(orecv_t[i], (dph[pl.ds(i * CH, CH)], dpl[pl.ds(i * CH, CH)])) for i in range(4)
    )

    def tall(unit, a, b, n):
        def part(i, _):
            lanes = pl.ds(pl.multiple_of(i * 128, 128), 128)
            value = (
                dot_tn(a[0][:, lanes], b[0][pl.ds(0, n)])
                + dot_tn(a[1][:, lanes], b[0][pl.ds(0, n)])
                + dot_tn(a[0][:, lanes], b[1][pl.ds(0, n)])
            )
            put(unit, value, i * 128)
            return 0

        lax.fori_loop(0, 4, part, 0)

    tall(UNITS["w2"], (hh, hl), (tabh, tabl), EDGES)
    rcut = split(rsum[...])
    put(UNITS["w1c"], three(dot_tn, node_pair(), rcut))
    next(rotations[0])
    next(rotations[1])
    tall(UNITS["w1b"], (sh, sl), (dph, dpl), EDGES)
    load_edge.wait()

    def cut_edges(i, _):
        r = rows(i * 128, 128)
        hi, lo = split(pre[r])
        hh[r] = hi
        hl[r] = lo
        return 0

    lax.fori_loop(0, 8, cut_edges, 0)
    tall(UNITS["w1a"], (hh, hl), (dph, dpl), EDGES)
    vectors = jnp.concatenate(
        [carry[1:2], carry[0:1], nb1_grad, ngain_grad, jnp.zeros((4, W), F32)], axis=0
    )
    small = UNITS["small"] * 512
    buf[small : small + 1024] = jnp.zeros((1024, 128), F32)
    for q in range(4):
        buf[small + 8 * q : small + 8 * q + 8] = vectors[:, q * 128 : q * 128 + 128]
    next(rotations[2])

    def edge_out(i, _):
        r = rows(i * CH, CH)
        ecot[r] += three(dot_nt, (dph[r], dpl[r]), weight("w1a"))
        return 0

    lax.fori_loop(0, EDGES // CH, edge_out, 0)
    store_edges = load(ecot, edge_grad_h, 13)
    ncot[...] += three(dot_nt, rcut, weight("w1c"))

    live = list(rotations)

    def step():
        for t in list(live):
            if next(t, 0) == 0:
                live.remove(t)

    for _ in range(BEFORE):
        step()
    wait(abuf.at[pl.ds(0, 1016)], recv2)

    def collect(i, _):
        gloc[...] += two(osend_t[i], split(abuf[rows(i * 256, 256)]))
        return 0

    lax.fori_loop(0, 4, collect, 0)
    ncot[...] += three(dot_nt, split(gloc[...]), weight("w1b"))
    store_grad = load(ncot, node_grad_h, 14)
    while live:
        step()
    stores = [store_nodes, store_edges, store_grad]
    k = 15
    for name, ref, at in (
        ("w1a", w1g_h, 0),
        ("w1b", w1g_h, 512),
        ("w1c", w1g_h, 1024),
        ("w2", w2g_h, 0),
        ("nw1a", nw1g_h, 0),
        ("nw1b", nw1g_h, 512),
        ("nw2", nw2g_h, 0),
    ):
        for q in range(4):
            src = out.at[pl.ds((UNITS[name] + q) * 512, 512)]
            stores.append(load(src, ref.at[pl.ds(at, 512), pl.ds(q * 128, 128)], k))
            k += 1
    for q in range(4):
        stores.append(load(out.at[pl.ds(small + 8 * q, 8)], small_h.at[:, pl.ds(q * 128, 128)], k))
        k += 1
    wait(sbuf.at[pl.ds(0, 1016)], send2)
    for d in started:
        d.wait_send()
    for d in stores:
        d.wait()


BEFORE = 4


def local(
    node_latent,
    edge_latent,
    edge_slot,
    edge_receiver,
    send_rows,
    node_cotangent,
    edge_cotangent,
    edge_w1,
    edge_b1,
    edge_w2,
    edge_gain,
    node_w1,
    node_b1,
    node_w2,
    node_gain,
):
    vectors = jnp.stack([edge_b1, edge_gain, node_b1, node_gain])
    shape = lambda *s: jax.ShapeDtypeStruct(s, F32)
    v32 = lambda *s: pltpu.VMEM(s, F32)
    v16 = lambda *s: pltpu.VMEM(s, BF16)
    anywhere = pl.BlockSpec(memory_space=pl.ANY)
    near = pl.BlockSpec(memory_space=pltpu.VMEM)
    result = pl.pallas_call(
        kernel,
        out_shape=(
            shape(NODES, W),
            shape(NODES, W),
            shape(EDGES, W),
            shape(1536, W),
            shape(512, W),
            shape(1024, W),
            shape(512, W),
            shape(8, W),
        ),
        in_specs=[near] * 4 + [anywhere] * 8,
        out_specs=[anywhere] * 8,
        scratch_shapes=[
            v32(NODES, W),
            v16(NODES, W),
            v16(NODES, W),
            v32(NODES, W),
            v32(EDGES, W),
            v32(EDGES, W),
            v16(3584, W),
            v16(3584, W),
            v32(EDGES, W),
            v32(EDGES, W),
            v32(EDGES, W),
            v16(EDGES, SLOTS),
            v16(EDGES, NODES),
            v16(4, NODES, 256),
            v16(EDGES, NODES),
            v16(4, NODES, 256),
            v16(SLOTS, W),
            v16(SLOTS, W),
            v16(EDGES, W),
            v16(EDGES, W),
            v16(EDGES, W),
            v16(EDGES, W),
            v16(EDGES, W),
            v16(EDGES, W),
            v32(EDGES, 128),
            v32(NODES, W),
            v32(NODES, W),
            v32(8, W),
            v32(NODES, W),
            v32(NODES, W),
            v32(FLAT, 128),
            v32(FLAT, 128),
            v32(3, 2520, 128),
            pltpu.SemaphoreType.DMA((48,)),
            pltpu.SemaphoreType.DMA,
            pltpu.SemaphoreType.DMA,
            pltpu.SemaphoreType.DMA,
            pltpu.SemaphoreType.DMA,
            pltpu.SemaphoreType.DMA((3, SEMS)),
            pltpu.SemaphoreType.DMA((3, SEMS)),
        ],
        compiler_params=pltpu.CompilerParams(
            collective_id=1, has_side_effects=True, vmem_limit_bytes=63 << 20
        ),
    )(
        edge_slot.reshape(8, 128),
        edge_receiver.reshape(8, 128),
        send_rows.reshape(8, 128),
        vectors,
        node_latent,
        edge_latent,
        node_cotangent,
        edge_cotangent,
        edge_w1,
        edge_w2,
        node_w1,
        node_w2,
    )
    new_nodes, node_grad, edge_grad, w1g, w2g, nw1g, nw2g, small = result
    return (
        new_nodes,
        node_grad,
        edge_grad,
        w1g,
        small[0],
        w2g,
        small[1],
        nw1g,
        small[2],
        nw2g,
        small[3],
    )


def solution(mesh):
    return jax.shard_map(
        local,
        mesh=mesh,
        in_specs=(
            P(("wide", "narrow"), None),
            P(("wide", "narrow"), None),
            P(("wide", "narrow")),
            P(("wide", "narrow")),
            P(("wide", "narrow"), None, None),
            P(("wide", "narrow"), None),
            P(("wide", "narrow"), None),
            P(),
            P(),
            P(),
            P(),
            P(),
            P(),
            P(),
            P(),
        ),
        out_specs=(
            P(("wide", "narrow"), None),
            P(("wide", "narrow"), None),
            P(("wide", "narrow"), None),
            P(),
            P(),
            P(),
            P(),
            P(),
            P(),
            P(),
            P(),
        ),
        check_vma=False,
    )
```

```python
import functools

import jax
import jax.numpy as jnp
from jax import lax
from jax.experimental import pallas as pl
from jax.experimental.pallas import tpu as pltpu
from jax.sharding import PartitionSpec as P

MESH = pl.DeviceIdType.MESH
F32, BF16, I32 = jnp.float32, jnp.bfloat16, jnp.int32
W = 512
NODES = 256
EDGES = 1024
SLOTS = 1280
CH = 256

FLAT = 15360
ORDERS = ((0, 1, 2), (1, 2, 0), (2, 0, 1))
SEMS = 30
PARTS = (
    (0, 0, 16, 0),
    (1, 2048, 16, 1008),
    (2, 4096, 16, 2016),
    (0, 6144, 24, 3024),
    (1, 9216, 24, 4536),
    (2, 12288, 24, 6048),
)
UNITS = {"nw2": 0, "nw1a": 4, "nw1b": 8, "w2": 12, "w1c": 16, "w1b": 20, "w1a": 24, "small": 28}
WROW = {"w1a": 0, "w1b": 512, "w1c": 1024, "w2": 1536, "nw1a": 2048, "nw1b": 2560, "nw2": 3072}


def coords():
    w = lax.axis_index("wide")
    n = lax.axis_index("narrow")
    return w % 4, n // 2, w // 4, n % 2


def device(x, y, z, c):
    return (z * 4 + x, y * 2 + c)


def wait(ref, sem):
    pltpu.make_async_copy(ref, ref, sem).wait()


def rows(start, n):
    return pl.ds(pl.multiple_of(start, 8), n)


def split(v):
    high = v.astype(BF16)
    return high, (v - high.astype(F32)).astype(BF16)


def dot(a, b):
    return jnp.dot(a, b, preferred_element_type=F32)


def dot_nt(a, b):
    return lax.dot_general(a, b, (((1,), (1,)), ((), ())), preferred_element_type=F32)


def dot_tn(a, b):
    return lax.dot_general(a, b, (((0,), (0,)), ((), ())), preferred_element_type=F32)


def three(op, a, b):
    return op(a[0], b[0]) + op(a[1], b[0]) + op(a[0], b[1])


def two(one_hot, pair):
    return dot(one_hot, pair[0]) + dot(one_hot, pair[1])


def reduce_part(part, buf, out, halves_in, send, recv, started):
    rot, base, leaf, into = PARTS[part]
    here = coords()
    core = here[3]
    order = ORDERS[rot]
    pos = [here[a] for a in order]
    sizes = (16 * leaf, 4 * leaf, leaf)

    def shifted(stage, by):
        c = list(here)
        c[order[stage]] = (c[order[stage]] + by) % 4
        return device(*c)

    sibling = device(here[0], here[1], here[2], 1 - core)

    def post(src, dst, k, to):
        d = pltpu.make_async_remote_copy(
            src_ref=src,
            dst_ref=dst,
            send_sem=send.at[part, k],
            recv_sem=recv.at[part, k],
            device_id=to,
            device_id_type=MESH,
        )
        d.start()
        started.append(d)

    mine = base + core * 64 * leaf
    other = base + (1 - core) * 64 * leaf
    L = sizes[0]
    A = L // 2
    j = pos[0]
    spot = lambda q: mine + ((j + q) % 4) * L
    for m, q in enumerate((2, -1, 1, 0)):
        r = rows(other + ((j + q) % 4) * L, L)
        post(buf.at[r], out.at[r], m, sibling)
    yield

    def core_add(m, q):
        wait(out.at[rows(spot(q), L)], recv.at[part, m])

        def add(i, _):
            r = rows(spot(q) + i * A, A)
            buf[r] = buf[r] + out[r]
            return 0

        lax.fori_loop(0, 2, add, 0)

    up, down = shifted(0, 1), shifted(0, -1)
    first_a, first_b = rows(into, A), rows(into + A, A)
    plus_a, plus_b = rows(into + L, A), rows(into + L + A, A)
    minus_a, minus_b = rows(into + 2 * L, A), rows(into + 2 * L + A, A)
    land = lambda r: halves_in.at[r]
    core_add(0, 2)
    post(buf.at[rows(spot(2), A)], land(first_a), 4, down)
    post(buf.at[rows(spot(2) + A, A)], land(first_b), 5, up)
    core_add(1, -1)
    post(buf.at[rows(spot(-1) + A, A)], land(plus_b), 6, down)
    core_add(2, 1)
    post(buf.at[rows(spot(1), A)], land(minus_a), 7, up)
    yield
    wait(land(first_a), recv.at[part, 4])
    r = rows(spot(-1), A)
    buf[r] = buf[r] + halves_in[first_a]
    post(buf.at[r], land(plus_a), 8, down)
    wait(land(first_b), recv.at[part, 5])
    r = rows(spot(1) + A, A)
    buf[r] = buf[r] + halves_in[first_b]
    post(buf.at[r], land(minus_b), 9, up)
    yield
    core_add(3, 0)
    wait(land(plus_b), recv.at[part, 6])
    wait(land(minus_a), recv.at[part, 7])
    wait(land(plus_a), recv.at[part, 8])
    wait(land(minus_b), recv.at[part, 9])
    r = rows(spot(0), L)
    buf[r] = buf[r] + halves_in[rows(into + L, L)] + halves_in[rows(into + 2 * L, L)]
    region = mine + j * L
    into += 3 * L
    for s in (1, 2):
        L = sizes[s]
        j = pos[s]
        k = 10 + 3 * (s - 1)
        for m, q in enumerate((2, 1, 3)):
            post(
                buf.at[rows(region + ((j + q) % 4) * L, L)],
                land(rows(into + m * L, L)),
                k + m,
                shifted(s, q),
            )
        yield
        for m in range(3):
            wait(land(rows(into + m * L, L)), recv.at[part, k + m])
        r = rows(region + j * L, L)
        total = buf[r] + halves_in[rows(into, L)]
        total = total + halves_in[rows(into + L, L)] + halves_in[rows(into + 2 * L, L)]
        if s == 1:
            buf[r] = total
        else:
            out[r] = total
        region = region + j * L
        into += 3 * L
    for s in (2, 1):
        L = sizes[s]
        j = pos[s]
        k = 16 + 3 * (2 - s)
        own = out.at[rows(region, L)]
        for m, q in enumerate((2, 1, 3)):
            post(own, own, k + m, shifted(s, q))
        yield
        region = region - j * L
        for m, q in enumerate((2, 3, 1)):
            wait(out.at[rows(region + ((j + q) % 4) * L, L)], recv.at[part, k + m])
    L = sizes[0]
    j = pos[0]
    own = out.at[rows(spot(0), L)]
    post(own, own, 22, up)
    post(own, own, 23, down)
    post(own, own, 26, sibling)
    yield
    left, right = out.at[rows(spot(-1), L)], out.at[rows(spot(1), L)]
    wait(left, recv.at[part, 22])
    piece = out.at[rows(spot(-1), A)]
    post(piece, piece, 24, up)
    post(left, left, 27, sibling)
    wait(right, recv.at[part, 23])
    piece = out.at[rows(spot(1) + A, A)]
    post(piece, piece, 25, down)
    post(right, right, 28, sibling)
    yield
    wait(out.at[rows(spot(2), A)], recv.at[part, 24])
    wait(out.at[rows(spot(2) + A, A)], recv.at[part, 25])
    opposite = out.at[rows(spot(2), L)]
    post(opposite, opposite, 29, sibling)
    yield
    for n in range(4):
        wait(out.at[rows(other, L)], recv.at[part, 26 + n])


def kernel(
    slot_ref, receiver_ref, list_ref, eb1_h, eg_h, nb1_h, ng_h,
    node_h, edge_h, ncot_h, ecot_h, w1_h, w2_h, nw1_h, nw2_h,
    new_nodes_h, node_grad_h, edge_grad_h, flat_h,
    vector_ref, node_v, node_hi, node_lo, ncot, ecot, pre, whi, wlo, sbuf, rbuf, abuf,
    oslot, orecv, orecv_t, osend, osend_t, tabh, tabl, sh, sl, hh, hl, dph, dpl,
    rstd_v, agg, npre, carry, gloc, rsum, buf, out, halves_in,
    lsem, send1, recv1, send2, recv2, send, recv,
):
    x, y, z, c = coords()
    me = (z * 4 + x) * 8 + y * 2 + c

    def peer(d):
        return (z + d // 32) % 4 * 4 + (x + d // 8) % 4, (y + d // 2) % 4 * 2 + (c + d) % 2

    def load(src, dst, k):
        d = pltpu.make_async_copy(src, dst, lsem.at[k])
        d.start()
        return d

    xhat = rbuf
    load_node = load(node_h, node_v, 0)
    load_vectors = [
        load(ref, vector_ref.at[i], 21 + i) for i, ref in enumerate((eb1_h, eg_h, nb1_h, ng_h))
    ]
    load_edge = load(edge_h, pre, 1)
    load_ncot = load(ncot_h, ncot, 2)
    blocks = [(w1_h, 0), (w1_h, 512), (w1_h, 1024), (w2_h, 0), (nw1_h, 0), (nw1_h, 512), (nw2_h, 0)]

    def load_weights(b):
        src, at = blocks[b]
        return load(src.at[pl.ds(at, 512)], ecot.at[pl.ds(b % 2 * 512, 512)], 3 + b)

    loading = {b: load_weights(b) for b in (0, 1)}
    barrier = pltpu.get_barrier_semaphore()

    def greet(i, _):
        for q in range(8):
            pl.semaphore_signal(barrier, inc=1, device_id=peer(i * 8 + q), device_id_type=MESH)
        return 0

    for i in range(1, 8):
        pl.semaphore_signal(barrier, inc=1, device_id=peer(i), device_id_type=MESH)
    lax.fori_loop(1, 16, greet, 0)

    def line(ref, i):
        return jnp.broadcast_to(ref[pl.ds(i, 1), :], (128, 128))

    def across(i, ref, store, n):
        lanes = lax.broadcasted_iota(I32, (128, 128), 1)
        column = line(ref, i).T
        for q in range(n // 128):
            store[rows(i * 128, 128), q * 128 : q * 128 + 128] = jnp.where(
                column == lanes + q * 128, 1.0, 0.0
            ).astype(BF16)

    def hot(i, _):
        across(i, list_ref, osend, NODES)
        return 0

    lax.fori_loop(0, 8, hot, 0)
    load_node.wait()
    for d in load_vectors:
        d.wait()
    nhi, nlo = split(node_v[...])
    node_hi[...] = nhi
    node_lo[...] = nlo

    def gather(i, _):
        r = rows(i * CH, CH)
        sbuf[r] = two(osend[r], (node_hi[...], node_lo[...]))
        return 0

    lax.fori_loop(0, EDGES // CH, gather, 0)
    mine8 = rows(me * 8, 8)
    rbuf[mine8] = sbuf[mine8]
    pl.semaphore_wait(barrier, 127)

    def send_rows(i, _):
        w, n = peer(i * 37 % 128)
        pltpu.make_async_remote_copy(
            src_ref=sbuf.at[rows((w * 8 + n) * 8, 8)],
            dst_ref=rbuf.at[mine8],
            send_sem=send1,
            recv_sem=recv1,
            device_id=(w, n),
            device_id_type=MESH,
        ).start()
        return 0

    lax.fori_loop(1, 128, send_rows, 0)

    for b in range(7):
        loading[b].wait()

        def cut(i, _, b=b):
            hi, lo = split(ecot[rows(b % 2 * 512 + i * 128, 128)])
            whi[rows(b * 512 + i * 128, 128)] = hi
            wlo[rows(b * 512 + i * 128, 128)] = lo
            return 0

        lax.fori_loop(0, 4, cut, 0)
        if b + 2 < 7:
            loading[b + 2] = load_weights(b + 2)
    load_ecot = load(ecot_h, ecot, 10)

    def weight(name):
        r = pl.ds(WROW[name], 512)
        return whi[r], wlo[r]

    def hot_edges(i, _):
        across(i, slot_ref, oslot, SLOTS)
        across(i, receiver_ref, orecv, NODES)
        return 0

    lax.fori_loop(0, 8, hot_edges, 0)

    def down(ref, i, first, n):
        return jnp.where(
            jnp.broadcast_to(ref[pl.ds(i, 1), :], (n, 128))
            == lax.broadcasted_iota(I32, (n, 128), 0) + first,
            1.0,
            0.0,
        ).astype(BF16)

    for i in range(8):
        lanes = slice(i % 2 * 128, i % 2 * 128 + 128)
        orecv_t[i // 2, :, lanes] = down(receiver_ref, i, 0, NODES)
        osend_t[i // 2, :, lanes] = down(list_ref, i, 0, NODES)

    node_pair = lambda: (node_hi[...], node_lo[...])
    projected = split(three(dot, node_pair(), weight("w1c")))
    agg[...] = projected[0].astype(F32)
    gloc[...] = projected[1].astype(F32)
    npre[...] = three(dot, node_pair(), weight("nw1a")) + vector_ref[2:3, :]
    load_edge.wait()

    def first_layer(i, _):
        r = rows(i * CH, CH)
        pair = split(pre[r])
        pre[r] = (
            three(dot, pair, weight("w1a"))
            + two(orecv[r], (agg[...].astype(BF16), gloc[...].astype(BF16)))
            + vector_ref[0:1, :]
        )
        return 0

    lax.fori_loop(0, EDGES // CH, first_layer, 0)
    tabh[0:NODES] = node_hi[...]
    tabl[0:NODES] = node_lo[...]
    agg[...] = jnp.zeros_like(agg)

    wait(rbuf.at[pl.ds(0, 1016)], recv1)
    wait(sbuf.at[pl.ds(0, 1016)], send1)

    def cut_table(i, _):
        hi, lo = split(rbuf[rows(i * 256, 256)])
        tabh[rows(256 + i * 256, 256)] = hi
        tabl[rows(256 + i * 256, 256)] = lo
        return 0

    lax.fori_loop(0, 4, cut_table, 0)

    def forward(i, _):
        r = rows(i * 512, 512)
        hot = oslot[r, 0:SLOTS]
        senders = dot(hot, tabh[...]).astype(BF16), dot(hot, tabl[...]).astype(BF16)
        sh[r] = senders[0]
        sl[r] = senders[1]
        v = pre[r] + three(dot, senders, weight("w1b"))
        s = 1.0 / (1.0 + jnp.exp(-v))
        pre[r] = s * (1.0 + v * (1.0 - s))
        hidden = split(v * s)
        hh[r] = hidden[0]
        hl[r] = hidden[1]
        zed = three(dot, hidden, weight("w2"))
        centre = zed - jnp.mean(zed, axis=1, keepdims=True)
        rstd = lax.rsqrt(jnp.mean(centre * centre, axis=1, keepdims=True) + 1e-05)
        scaled = centre * rstd
        xhat[r] = scaled
        rstd_v[r] = jnp.broadcast_to(rstd, (512, 128))
        pair = split(scaled)
        agg[...] += two(orecv_t[2 * i], (pair[0][:256], pair[1][:256]))
        agg[...] += two(orecv_t[2 * i + 1], (pair[0][256:], pair[1][256:]))
        return 0

    lax.fori_loop(0, 2, forward, 0)

    aggregate = split(agg[...] * vector_ref[1:2, :])
    v = npre[...] + three(dot, aggregate, weight("nw1b"))
    s = 1.0 / (1.0 + jnp.exp(-v))
    slope = s * (1.0 + v * (1.0 - s))
    hidden = split(v * s)
    zed = three(dot, hidden, weight("nw2"))
    centre = zed - jnp.mean(zed, axis=1, keepdims=True)
    rstd = lax.rsqrt(jnp.mean(centre * centre, axis=1, keepdims=True) + 1e-05)
    scaled = centre * rstd
    npre[...] = node_v[...] + scaled * vector_ref[3:4, :]
    store_nodes = load(npre, new_nodes_h, 11)
    load_ncot.wait()
    ngain_grad = jnp.sum(ncot[...] * scaled, axis=0, keepdims=True)
    cot = ncot[...] * vector_ref[3:4, :]
    dz = split(
        rstd
        * (
            cot
            - jnp.mean(cot, axis=1, keepdims=True)
            - scaled * jnp.mean(cot * scaled, axis=1, keepdims=True)
        )
    )
    dpre = three(dot_nt, dz, weight("nw2")) * slope
    nb1_grad = jnp.sum(dpre, axis=0, keepdims=True)
    dpre = split(dpre)
    dagg = split(three(dot_nt, dpre, weight("nw1b")))

    def put(unit, value, first=0):
        for q in range(4):
            buf[rows((unit + q) * 512 + first, value.shape[0])] = value[:, q * 128 : q * 128 + 128]

    put(UNITS["nw2"], three(dot_tn, hidden, dz))
    put(UNITS["nw1a"], three(dot_tn, node_pair(), dpre))
    put(UNITS["nw1b"], three(dot_tn, aggregate, dpre))
    started = []
    parts = [reduce_part(p, buf, out, halves_in, send, recv, started) for p in range(6)]
    stores = [store_nodes]
    due = list(range(6))

    def step(first, last):
        for p in range(first, last):
            if p in due and next(parts[p], 0) == 0:
                due.remove(p)
                r = pl.ds(PARTS[p][1], 128 * PARTS[p][2])
                stores.append(load(out.at[r], flat_h.at[r], 15 + p))

    def act(tokens):
        for t in tokens:
            if t == "E":
                step(0, 3)
            elif t == "L":
                step(3, 6)
            elif t[0] == "p":
                step(int(t[1]), int(t[1]) + 1)
            elif t[0] == "B":
                n = int(t[1])
                give(max(1, 16 * n), 16 * n + 16)
            elif t == "edges":
                finish_edges()
            else:
                finish_nodes()

    act(PLAN[0])

    load_ecot.wait()
    carry[...] = jnp.zeros_like(carry)
    agg[...] = dagg[0].astype(F32)
    gloc[...] = dagg[1].astype(F32)

    def backward(i, _):
        r = rows(i * 512, 512)
        scaled = xhat[r]
        mcot = ecot[r] + two(orecv[r], (agg[...].astype(BF16), gloc[...].astype(BF16)))
        carry[0:1] += jnp.sum(mcot * scaled, axis=0, keepdims=True)
        cot = mcot * vector_ref[1:2, :]
        dz = split(
            rstd_v[r][:, 0:1]
            * (
                cot
                - jnp.mean(cot, axis=1, keepdims=True)
                - scaled * jnp.mean(cot * scaled, axis=1, keepdims=True)
            )
        )
        tabh[r] = dz[0]
        tabl[r] = dz[1]
        dpre = three(dot_nt, dz, weight("w2")) * pre[r]
        carry[1:2] += jnp.sum(dpre, axis=0, keepdims=True)
        dpre = split(dpre)
        dph[r] = dpre[0]
        dpl[r] = dpre[1]
        return 0

    lax.fori_loop(0, 2, backward, 0)
    act(PLAN[1])
    load_edge = load(edge_h, pre, 12)

    def scatter(first):
        for i in range(8):
            oslot[0:256, i * 128 : i * 128 + 128] = down(slot_ref, i, first, 256)
        return two(oslot[0:256, 0:EDGES], (dph[...], dpl[...]))

    def plane(n, _):
        at = (z + n) % 4 * 256
        sbuf[rows(at, 256)] = scatter(NODES + at)
        return 0

    def give(first, last):
        def one(i, _):
            w, nn = peer(i * 37 % 128)
            pltpu.make_async_remote_copy(
                src_ref=sbuf.at[rows((w * 8 + nn) * 8, 8)],
                dst_ref=abuf.at[mine8],
                send_sem=send2,
                recv_sem=recv2,
                device_id=(w, nn),
                device_id_type=MESH,
            ).start()
            return 0

        lax.fori_loop(first, last, one, 0)

    lax.fori_loop(0, 4, plane, 0)
    act(PLAN[2])
    abuf[mine8] = sbuf[mine8]
    gloc[...] = scatter(0)
    rsum[...] = sum(
        two(orecv_t[i], (dph[pl.ds(i * CH, CH)], dpl[pl.ds(i * CH, CH)])) for i in range(4)
    )

    def tall(unit, a, b, n):
        def part(i, _):
            lanes = pl.ds(pl.multiple_of(i * 128, 128), 128)
            value = (
                dot_tn(a[0][:, lanes], b[0][pl.ds(0, n)])
                + dot_tn(a[1][:, lanes], b[0][pl.ds(0, n)])
                + dot_tn(a[0][:, lanes], b[1][pl.ds(0, n)])
            )
            put(unit, value, i * 128)
            return 0

        lax.fori_loop(0, 4, part, 0)

    tall(UNITS["w2"], (hh, hl), (tabh, tabl), EDGES)
    act(PLAN[3])
    rcut = split(rsum[...])
    put(UNITS["w1c"], three(dot_tn, node_pair(), rcut))
    act(PLAN[4])
    tall(UNITS["w1b"], (sh, sl), (dph, dpl), EDGES)
    act(PLAN[5])
    load_edge.wait()

    def cut_edges(i, _):
        r = rows(i * 128, 128)
        hi, lo = split(pre[r])
        hh[r] = hi
        hl[r] = lo
        return 0

    lax.fori_loop(0, 8, cut_edges, 0)
    tall(UNITS["w1a"], (hh, hl), (dph, dpl), EDGES)
    vectors = jnp.concatenate(
        [carry[1:2], carry[0:1], nb1_grad, ngain_grad, jnp.zeros((4, W), F32)], axis=0
    )
    small = UNITS["small"] * 512
    buf[small : small + 1024] = jnp.zeros((1024, 128), F32)
    for q in range(4):
        buf[small + 8 * q : small + 8 * q + 8] = vectors[:, q * 128 : q * 128 + 128]

    def edge_out(i, _):
        r = rows(i * CH, CH)
        ecot[r] += three(dot_nt, (dph[r], dpl[r]), weight("w1a"))
        return 0

    def finish_edges():
        lax.fori_loop(0, EDGES // CH, edge_out, 0)
        stores.append(load(ecot, edge_grad_h, 13))
        ncot[...] += three(dot_nt, rcut, weight("w1c")) + three(dot_nt, dpre, weight("nw1a"))

    def collect(i, _):
        gloc[...] += two(osend_t[i], split(abuf[rows(i * 256, 256)]))
        return 0

    def finish_nodes():
        wait(abuf.at[pl.ds(0, 1016)], recv2)
        lax.fori_loop(0, 4, collect, 0)
        ncot[...] += three(dot_nt, split(gloc[...]), weight("w1b"))
        stores.append(load(ncot, node_grad_h, 14))

    act(PLAN[6])
    while due:
        step(0, 6)
    wait(sbuf.at[pl.ds(0, 1016)], send2)
    for d in started:
        d.wait_send()
    for d in stores:
        d.wait()


PLAN = (
    ("E",),
    ("E",),
    ("B0",),
    ("E", "B1",),
    ("p3",),
    ("E", "B2", "p4",),
    ("p5", "E", "B3", "edges", "E", "B4", "L", "E", "B5", "L", "E", "B6", "L", "E", "B7", "L", "E", "L", "nodes",),
)


def place(*refs):
    source, target, sems = refs[:4], refs[4:15], refs[15:17]
    flat, near = refs[17], refs[18:]
    moves = []

    def move(src, mid, dst):
        n = len(moves)
        moves.append(
            (
                pltpu.make_async_copy(src, mid, sems[0].at[n]),
                pltpu.make_async_copy(mid, dst, sems[1].at[n]),
            )
        )
        moves[-1][0].start()

    first = UNITS["small"] * 512
    for i, k in enumerate((4, 6, 8, 10)):
        for q in range(4):
            r = first + 8 * q + i
            move(source[3].at[r], flat.at[r], target[k].at[pl.ds(q * 128, 128)])
    for k in range(3):
        move(source[k], near[k], target[k])
    for name, k, at in (
        ("w1a", 3, 0),
        ("w1b", 3, 512),
        ("w1c", 3, 1024),
        ("w2", 5, 0),
        ("nw1a", 7, 0),
        ("nw1b", 7, 512),
        ("nw2", 9, 0),
    ):
        for q in range(4):
            r = pl.ds((UNITS[name] + q) * 512, 512)
            move(
                source[3].at[r], flat.at[r], target[k].at[pl.ds(at, 512), pl.ds(q * 128, 128)]
            )
    for inward, outward in moves:
        inward.wait()
        outward.start()
    for inward, outward in moves:
        outward.wait()


def local(
    node_latent,
    edge_latent,
    edge_slot,
    edge_receiver,
    send_rows,
    node_cotangent,
    edge_cotangent,
    edge_w1,
    edge_b1,
    edge_w2,
    edge_gain,
    node_w1,
    node_b1,
    node_w2,
    node_gain,
):
    shape = lambda *s: jax.ShapeDtypeStruct(s, F32)
    v32 = lambda *s: pltpu.VMEM(s, F32)
    v16 = lambda *s: pltpu.VMEM(s, BF16)
    anywhere = pl.BlockSpec(memory_space=pl.ANY)
    near = pl.BlockSpec(memory_space=pltpu.VMEM)
    result = pl.pallas_call(
        kernel,
        out_shape=(
            shape(NODES, W),
            shape(NODES, W),
            shape(EDGES, W),
            shape(FLAT, 128),
        ),
        in_specs=[near] * 3 + [anywhere] * 12,
        out_specs=[anywhere] * 4,
        scratch_shapes=[
            v32(4, W),
            v32(NODES, W),
            v16(NODES, W),
            v16(NODES, W),
            v32(NODES, W),
            v32(EDGES, W),
            v32(EDGES, W),
            v16(3584, W),
            v16(3584, W),
            v32(EDGES, W),
            v32(EDGES, W),
            v32(EDGES, W),
            v16(EDGES, SLOTS),
            v16(EDGES, NODES),
            v16(4, NODES, 256),
            v16(EDGES, NODES),
            v16(4, NODES, 256),
            v16(SLOTS, W),
            v16(SLOTS, W),
            v16(EDGES, W),
            v16(EDGES, W),
            v16(EDGES, W),
            v16(EDGES, W),
            v16(EDGES, W),
            v16(EDGES, W),
            v32(EDGES, 128),
            v32(NODES, W),
            v32(NODES, W),
            v32(8, W),
            v32(NODES, W),
            v32(NODES, W),
            v32(FLAT, 128),
            v32(FLAT, 128),
            v32(7560, 128),
            pltpu.SemaphoreType.DMA((32,)),
            pltpu.SemaphoreType.DMA,
            pltpu.SemaphoreType.DMA,
            pltpu.SemaphoreType.DMA,
            pltpu.SemaphoreType.DMA,
            pltpu.SemaphoreType.DMA((6, SEMS)),
            pltpu.SemaphoreType.DMA((6, SEMS)),
        ],
        compiler_params=pltpu.CompilerParams(
            collective_id=1, has_side_effects=True, vmem_limit_bytes=63 << 20
        ),
    )(
        edge_slot.reshape(8, 128),
        edge_receiver.reshape(8, 128),
        send_rows.reshape(8, 128),
        edge_b1,
        edge_gain,
        node_b1,
        node_gain,
        node_latent,
        edge_latent,
        node_cotangent,
        edge_cotangent,
        edge_w1,
        edge_w2,
        node_w1,
        node_w2,
    )
    return pl.pallas_call(
        place,
        out_shape=(
            shape(NODES, W),
            shape(NODES, W),
            shape(EDGES, W),
            shape(1536, W),
            shape(512),
            shape(512, W),
            shape(512),
            shape(1024, W),
            shape(512),
            shape(512, W),
            shape(512),
        ),
        in_specs=[anywhere] * 4,
        out_specs=(anywhere,) * 11,
        scratch_shapes=[
            pltpu.SemaphoreType.DMA((47,)),
            pltpu.SemaphoreType.DMA((47,)),
            v32(FLAT, 128),
            v32(NODES, W),
            v32(NODES, W),
            v32(EDGES, W),
        ],
        compiler_params=pltpu.CompilerParams(vmem_limit_bytes=60 << 20),
    )(*result)


def solution(mesh):
    return jax.shard_map(
        local,
        mesh=mesh,
        in_specs=(
            P(("wide", "narrow"), None),
            P(("wide", "narrow"), None),
            P(("wide", "narrow")),
            P(("wide", "narrow")),
            P(("wide", "narrow"), None, None),
            P(("wide", "narrow"), None),
            P(("wide", "narrow"), None),
            P(),
            P(),
            P(),
            P(),
            P(),
            P(),
            P(),
            P(),
        ),
        out_specs=(
            P(("wide", "narrow"), None),
            P(("wide", "narrow"), None),
            P(("wide", "narrow"), None),
            P(),
            P(),
            P(),
            P(),
            P(),
            P(),
            P(),
            P(),
        ),
        check_vma=False,
    )
```

```python
import functools

import jax
import jax.numpy as jnp
from jax import lax
from jax.experimental import pallas as pl
from jax.experimental.pallas import tpu as pltpu
from jax.sharding import PartitionSpec as P

MESH = pl.DeviceIdType.MESH
F32, BF16, I32 = jnp.float32, jnp.bfloat16, jnp.int32
W = 512
NODES = 256
EDGES = 1024
SLOTS = 1280
CH = 256

FLAT = 15360
ORDERS = ((0, 1, 2), (1, 2, 0), (2, 0, 1))
SEMS = 30
PARTS = (
    (0, 0, 16, 0),
    (1, 2048, 16, 1008),
    (2, 4096, 16, 2016),
    (0, 6144, 24, 3024),
    (1, 9216, 24, 4536),
    (2, 12288, 24, 6048),
)
UNITS = {"nw2": 0, "nw1a": 4, "nw1b": 8, "w2": 12, "w1c": 16, "w1b": 20, "w1a": 24, "small": 28}
WROW = {"w1a": 0, "w1b": 512, "w1c": 1024, "w2": 1536, "nw1a": 2048, "nw1b": 2560, "nw2": 3072}


def coords():
    w = lax.axis_index("wide")
    n = lax.axis_index("narrow")
    return w % 4, n // 2, w // 4, n % 2


def device(x, y, z, c):
    return (z * 4 + x, y * 2 + c)


def wait(ref, sem):
    pltpu.make_async_copy(ref, ref, sem).wait()


def rows(start, n):
    return pl.ds(pl.multiple_of(start, 8), n)


def split(v):
    high = v.astype(BF16)
    return high, (v - high.astype(F32)).astype(BF16)


def dot(a, b):
    return jnp.dot(a, b, preferred_element_type=F32)


def dot_nt(a, b):
    return lax.dot_general(a, b, (((1,), (1,)), ((), ())), preferred_element_type=F32)


def dot_tn(a, b):
    return lax.dot_general(a, b, (((0,), (0,)), ((), ())), preferred_element_type=F32)


def three(op, a, b):
    return op(a[0], b[0]) + op(a[1], b[0]) + op(a[0], b[1])


def two(one_hot, pair):
    return dot(one_hot, pair[0]) + dot(one_hot, pair[1])


def reduce_part(part, buf, out, halves_in, send, recv, started):
    rot, base, leaf, into = PARTS[part]
    here = coords()
    core = here[3]
    order = ORDERS[rot]
    pos = [here[a] for a in order]
    sizes = (16 * leaf, 4 * leaf, leaf)

    def shifted(stage, by):
        c = list(here)
        c[order[stage]] = (c[order[stage]] + by) % 4
        return device(*c)

    sibling = device(here[0], here[1], here[2], 1 - core)

    def post(src, dst, k, to):
        d = pltpu.make_async_remote_copy(
            src_ref=src,
            dst_ref=dst,
            send_sem=send.at[part, k],
            recv_sem=recv.at[part, k],
            device_id=to,
            device_id_type=MESH,
        )
        d.start()
        started.append(d)

    mine = base + core * 64 * leaf
    other = base + (1 - core) * 64 * leaf
    L = sizes[0]
    A = L // 2
    j = pos[0]
    spot = lambda q: mine + ((j + q) % 4) * L
    for m, q in enumerate((2, -1, 1, 0)):
        r = rows(other + ((j + q) % 4) * L, L)
        post(buf.at[r], out.at[r], m, sibling)
    yield

    def core_add(m, q):
        wait(out.at[rows(spot(q), L)], recv.at[part, m])

        def add(i, _):
            r = rows(spot(q) + i * A, A)
            buf[r] = buf[r] + out[r]
            return 0

        lax.fori_loop(0, 2, add, 0)

    up, down = shifted(0, 1), shifted(0, -1)
    first_a, first_b = rows(into, A), rows(into + A, A)
    plus_a, plus_b = rows(into + L, A), rows(into + L + A, A)
    minus_a, minus_b = rows(into + 2 * L, A), rows(into + 2 * L + A, A)
    land = lambda r: halves_in.at[r]
    core_add(0, 2)
    post(buf.at[rows(spot(2), A)], land(first_a), 4, down)
    post(buf.at[rows(spot(2) + A, A)], land(first_b), 5, up)
    core_add(1, -1)
    post(buf.at[rows(spot(-1) + A, A)], land(plus_b), 6, down)
    core_add(2, 1)
    post(buf.at[rows(spot(1), A)], land(minus_a), 7, up)
    yield
    wait(land(first_a), recv.at[part, 4])
    r = rows(spot(-1), A)
    buf[r] = buf[r] + halves_in[first_a]
    post(buf.at[r], land(plus_a), 8, down)
    wait(land(first_b), recv.at[part, 5])
    r = rows(spot(1) + A, A)
    buf[r] = buf[r] + halves_in[first_b]
    post(buf.at[r], land(minus_b), 9, up)
    yield
    core_add(3, 0)
    wait(land(plus_b), recv.at[part, 6])
    wait(land(minus_a), recv.at[part, 7])
    wait(land(plus_a), recv.at[part, 8])
    wait(land(minus_b), recv.at[part, 9])
    r = rows(spot(0), L)
    buf[r] = buf[r] + halves_in[rows(into + L, L)] + halves_in[rows(into + 2 * L, L)]
    region = mine + j * L
    into += 3 * L
    for s in (1, 2):
        L = sizes[s]
        j = pos[s]
        k = 10 + 3 * (s - 1)
        for m, q in enumerate((2, 1, 3)):
            post(
                buf.at[rows(region + ((j + q) % 4) * L, L)],
                land(rows(into + m * L, L)),
                k + m,
                shifted(s, q),
            )
        yield
        for m in range(3):
            wait(land(rows(into + m * L, L)), recv.at[part, k + m])
        r = rows(region + j * L, L)
        total = buf[r] + halves_in[rows(into, L)]
        total = total + halves_in[rows(into + L, L)] + halves_in[rows(into + 2 * L, L)]
        if s == 1:
            buf[r] = total
        else:
            out[r] = total
        region = region + j * L
        into += 3 * L
    for s in (2, 1):
        L = sizes[s]
        j = pos[s]
        k = 16 + 3 * (2 - s)
        own = out.at[rows(region, L)]
        for m, q in enumerate((2, 1, 3)):
            post(own, own, k + m, shifted(s, q))
        yield
        region = region - j * L
        for m, q in enumerate((2, 3, 1)):
            wait(out.at[rows(region + ((j + q) % 4) * L, L)], recv.at[part, k + m])
    L = sizes[0]
    j = pos[0]
    own = out.at[rows(spot(0), L)]
    post(own, own, 22, up)
    post(own, own, 23, down)
    post(own, own, 26, sibling)
    yield
    left, right = out.at[rows(spot(-1), L)], out.at[rows(spot(1), L)]
    wait(left, recv.at[part, 22])
    piece = out.at[rows(spot(-1), A)]
    post(piece, piece, 24, up)
    post(left, left, 27, sibling)
    wait(right, recv.at[part, 23])
    piece = out.at[rows(spot(1) + A, A)]
    post(piece, piece, 25, down)
    post(right, right, 28, sibling)
    yield
    wait(out.at[rows(spot(2), A)], recv.at[part, 24])
    wait(out.at[rows(spot(2) + A, A)], recv.at[part, 25])
    opposite = out.at[rows(spot(2), L)]
    post(opposite, opposite, 29, sibling)
    yield
    for n in range(4):
        wait(out.at[rows(other, L)], recv.at[part, 26 + n])


def kernel(
    slot_ref, receiver_ref, list_ref, eb1_h, eg_h, nb1_h, ng_h,
    node_h, edge_h, ncot_h, ecot_h, w1_h, w2_h, nw1_h, nw2_h,
    new_nodes_h, node_grad_h, edge_grad_h, flat_h,
    vector_ref, node_v, node_hi, node_lo, ncot, ecot, pre, whi, wlo, sbuf, rbuf, abuf,
    oslot, orecv, orecv_t, osend, osend_t, tabh, tabl, sh, sl, hh, hl, dph, dpl,
    rstd_v, agg, npre, carry, gloc, rsum, buf, out, halves_in,
    lsem, send1, recv1, send2, recv2, send, recv,
):
    x, y, z, c = coords()
    me = (z * 4 + x) * 8 + y * 2 + c

    def peer(d):
        return (z + d // 32) % 4 * 4 + (x + d // 8) % 4, (y + d // 2) % 4 * 2 + (c + d) % 2

    def load(src, dst, k):
        d = pltpu.make_async_copy(src, dst, lsem.at[k])
        d.start()
        return d

    xhat = rbuf
    load_node = load(node_h, node_v, 0)
    load_vectors = [
        load(ref, vector_ref.at[i], 21 + i) for i, ref in enumerate((eb1_h, eg_h, nb1_h, ng_h))
    ]
    load_edge = load(edge_h, pre, 1)
    load_ncot = load(ncot_h, ncot, 2)
    blocks = [(w1_h, 0), (w1_h, 512), (w1_h, 1024), (w2_h, 0), (nw1_h, 0), (nw1_h, 512), (nw2_h, 0)]

    def load_weights(b):
        src, at = blocks[b]
        return load(src.at[pl.ds(at, 512)], ecot.at[pl.ds(b % 2 * 512, 512)], 3 + b)

    loading = {b: load_weights(b) for b in (0, 1)}
    barrier = pltpu.get_barrier_semaphore()

    def greet(i, _):
        for q in range(8):
            pl.semaphore_signal(barrier, inc=1, device_id=peer(i * 8 + q), device_id_type=MESH)
        return 0

    for i in range(1, 8):
        pl.semaphore_signal(barrier, inc=1, device_id=peer(i), device_id_type=MESH)
    lax.fori_loop(1, 16, greet, 0)

    def line(ref, i):
        return jnp.broadcast_to(ref[pl.ds(i, 1), :], (128, 128))

    def across(i, ref, store, n):
        lanes = lax.broadcasted_iota(I32, (128, 128), 1)
        column = line(ref, i).T
        for q in range(n // 128):
            store[rows(i * 128, 128), q * 128 : q * 128 + 128] = jnp.where(
                column == lanes + q * 128, 1.0, 0.0
            ).astype(BF16)

    def hot(i, _):
        across(i, list_ref, osend, NODES)
        return 0

    lax.fori_loop(0, 8, hot, 0)
    load_node.wait()
    for d in load_vectors:
        d.wait()
    nhi, nlo = split(node_v[...])
    node_hi[...] = nhi
    node_lo[...] = nlo

    def gather(i, _):
        r = rows(i * CH, CH)
        sbuf[r] = two(osend[r], (node_hi[...], node_lo[...]))
        return 0

    lax.fori_loop(0, EDGES // CH, gather, 0)
    mine8 = rows(me * 8, 8)
    rbuf[mine8] = sbuf[mine8]
    pl.semaphore_wait(barrier, 127)

    def send_rows(i, _):
        w, n = peer(i * 37 % 128)
        pltpu.make_async_remote_copy(
            src_ref=sbuf.at[rows((w * 8 + n) * 8, 8)],
            dst_ref=rbuf.at[mine8],
            send_sem=send1,
            recv_sem=recv1,
            device_id=(w, n),
            device_id_type=MESH,
        ).start()
        return 0

    lax.fori_loop(1, 128, send_rows, 0)

    for b in range(7):
        loading[b].wait()

        def cut(i, _, b=b):
            hi, lo = split(ecot[rows(b % 2 * 512 + i * 128, 128)])
            whi[rows(b * 512 + i * 128, 128)] = hi
            wlo[rows(b * 512 + i * 128, 128)] = lo
            return 0

        lax.fori_loop(0, 4, cut, 0)
        if b + 2 < 7:
            loading[b + 2] = load_weights(b + 2)
    load_ecot = load(ecot_h, ecot, 10)

    def weight(name):
        r = pl.ds(WROW[name], 512)
        return whi[r], wlo[r]

    def hot_edges(i, _):
        across(i, slot_ref, oslot, SLOTS)
        across(i, receiver_ref, orecv, NODES)
        return 0

    lax.fori_loop(0, 8, hot_edges, 0)

    def down(ref, i, first, n):
        return jnp.where(
            jnp.broadcast_to(ref[pl.ds(i, 1), :], (n, 128))
            == lax.broadcasted_iota(I32, (n, 128), 0) + first,
            1.0,
            0.0,
        ).astype(BF16)

    for i in range(8):
        lanes = slice(i % 2 * 128, i % 2 * 128 + 128)
        orecv_t[i // 2, :, lanes] = down(receiver_ref, i, 0, NODES)
        osend_t[i // 2, :, lanes] = down(list_ref, i, 0, NODES)

    node_pair = lambda: (node_hi[...], node_lo[...])
    projected = split(three(dot, node_pair(), weight("w1c")))
    agg[...] = projected[0].astype(F32)
    gloc[...] = projected[1].astype(F32)
    npre[...] = three(dot, node_pair(), weight("nw1a")) + vector_ref[2:3, :]
    load_edge.wait()

    def first_layer(i, _):
        r = rows(i * CH, CH)
        pair = split(pre[r])
        pre[r] = (
            three(dot, pair, weight("w1a"))
            + two(orecv[r], (agg[...].astype(BF16), gloc[...].astype(BF16)))
            + vector_ref[0:1, :]
        )
        return 0

    lax.fori_loop(0, EDGES // CH, first_layer, 0)
    tabh[0:NODES] = node_hi[...]
    tabl[0:NODES] = node_lo[...]
    agg[...] = jnp.zeros_like(agg)

    wait(rbuf.at[pl.ds(0, 1016)], recv1)
    wait(sbuf.at[pl.ds(0, 1016)], send1)

    def cut_table(i, _):
        hi, lo = split(rbuf[rows(i * 256, 256)])
        tabh[rows(256 + i * 256, 256)] = hi
        tabl[rows(256 + i * 256, 256)] = lo
        return 0

    lax.fori_loop(0, 4, cut_table, 0)

    def forward(i, _):
        r = rows(i * 512, 512)
        hot = oslot[r, 0:SLOTS]
        senders = dot(hot, tabh[...]).astype(BF16), dot(hot, tabl[...]).astype(BF16)
        sh[r] = senders[0]
        sl[r] = senders[1]
        v = pre[r] + three(dot, senders, weight("w1b"))
        s = 1.0 / (1.0 + jnp.exp(-v))
        pre[r] = s * (1.0 + v * (1.0 - s))
        hidden = split(v * s)
        hh[r] = hidden[0]
        hl[r] = hidden[1]
        zed = three(dot, hidden, weight("w2"))
        centre = zed - jnp.mean(zed, axis=1, keepdims=True)
        rstd = lax.rsqrt(jnp.mean(centre * centre, axis=1, keepdims=True) + 1e-05)
        scaled = centre * rstd
        xhat[r] = scaled
        rstd_v[r] = jnp.broadcast_to(rstd, (512, 128))
        pair = split(scaled)
        agg[...] += two(orecv_t[2 * i], (pair[0][:256], pair[1][:256]))
        agg[...] += two(orecv_t[2 * i + 1], (pair[0][256:], pair[1][256:]))
        return 0

    lax.fori_loop(0, 2, forward, 0)

    aggregate = split(agg[...] * vector_ref[1:2, :])
    v = npre[...] + three(dot, aggregate, weight("nw1b"))
    s = 1.0 / (1.0 + jnp.exp(-v))
    slope = s * (1.0 + v * (1.0 - s))
    hidden = split(v * s)
    zed = three(dot, hidden, weight("nw2"))
    centre = zed - jnp.mean(zed, axis=1, keepdims=True)
    rstd = lax.rsqrt(jnp.mean(centre * centre, axis=1, keepdims=True) + 1e-05)
    scaled = centre * rstd
    npre[...] = node_v[...] + scaled * vector_ref[3:4, :]
    store_nodes = load(npre, new_nodes_h, 11)
    load_ncot.wait()
    ngain_grad = jnp.sum(ncot[...] * scaled, axis=0, keepdims=True)
    cot = ncot[...] * vector_ref[3:4, :]
    dz = split(
        rstd
        * (
            cot
            - jnp.mean(cot, axis=1, keepdims=True)
            - scaled * jnp.mean(cot * scaled, axis=1, keepdims=True)
        )
    )
    dpre = three(dot_nt, dz, weight("nw2")) * slope
    nb1_grad = jnp.sum(dpre, axis=0, keepdims=True)
    dpre = split(dpre)
    dagg = split(three(dot_nt, dpre, weight("nw1b")))

    def put(unit, value, first=0):
        for q in range(4):
            buf[rows((unit + q) * 512 + first, value.shape[0])] = value[:, q * 128 : q * 128 + 128]

    put(UNITS["nw2"], three(dot_tn, hidden, dz))
    put(UNITS["nw1a"], three(dot_tn, node_pair(), dpre))
    put(UNITS["nw1b"], three(dot_tn, aggregate, dpre))
    started = []
    parts = [reduce_part(p, buf, out, halves_in, send, recv, started) for p in range(6)]
    stores = [store_nodes]
    due = list(range(6))

    def step(first, last):
        for p in range(first, last):
            if p in due and next(parts[p], 0) == 0:
                due.remove(p)
                r = pl.ds(PARTS[p][1], 128 * PARTS[p][2])
                stores.append(load(out.at[r], flat_h.at[r], 15 + p))

    def act(tokens):
        for t in tokens:
            if t == "E":
                step(0, 3)
            elif t == "L":
                step(3, 6)
            elif t[0] == "p":
                step(int(t[1]), int(t[1]) + 1)
            elif t[0] == "B":
                n = int(t[1])
                give(max(1, 16 * n), 16 * n + 16)
            elif t == "edges":
                finish_edges()
            else:
                finish_nodes()

    act(PLAN[0])

    load_ecot.wait()
    carry[...] = jnp.zeros_like(carry)
    agg[...] = dagg[0].astype(F32)
    gloc[...] = dagg[1].astype(F32)

    def backward(i, _):
        r = rows(i * 512, 512)
        scaled = xhat[r]
        mcot = ecot[r] + two(orecv[r], (agg[...].astype(BF16), gloc[...].astype(BF16)))
        carry[0:1] += jnp.sum(mcot * scaled, axis=0, keepdims=True)
        cot = mcot * vector_ref[1:2, :]
        dz = split(
            rstd_v[r][:, 0:1]
            * (
                cot
                - jnp.mean(cot, axis=1, keepdims=True)
                - scaled * jnp.mean(cot * scaled, axis=1, keepdims=True)
            )
        )
        tabh[r] = dz[0]
        tabl[r] = dz[1]
        dpre = three(dot_nt, dz, weight("w2")) * pre[r]
        carry[1:2] += jnp.sum(dpre, axis=0, keepdims=True)
        dpre = split(dpre)
        dph[r] = dpre[0]
        dpl[r] = dpre[1]
        return 0

    lax.fori_loop(0, 2, backward, 0)
    act(PLAN[1])
    load_edge = load(edge_h, pre, 12)

    def scatter(first):
        for i in range(8):
            oslot[0:256, i * 128 : i * 128 + 128] = down(slot_ref, i, first, 256)
        return two(oslot[0:256, 0:EDGES], (dph[...], dpl[...]))

    def plane(n, _):
        at = (z + n) % 4 * 256
        sbuf[rows(at, 256)] = scatter(NODES + at)
        return 0

    def give(first, last):
        def one(i, _):
            w, nn = peer(i * 37 % 128)
            pltpu.make_async_remote_copy(
                src_ref=sbuf.at[rows((w * 8 + nn) * 8, 8)],
                dst_ref=abuf.at[mine8],
                send_sem=send2,
                recv_sem=recv2,
                device_id=(w, nn),
                device_id_type=MESH,
            ).start()
            return 0

        lax.fori_loop(first, last, one, 0)

    lax.fori_loop(0, 4, plane, 0)
    act(PLAN[2])
    abuf[mine8] = sbuf[mine8]
    gloc[...] = scatter(0)
    rsum[...] = sum(
        two(orecv_t[i], (dph[pl.ds(i * CH, CH)], dpl[pl.ds(i * CH, CH)])) for i in range(4)
    )

    def tall(unit, a, b, n):
        def part(i, _):
            lanes = pl.ds(pl.multiple_of(i * 128, 128), 128)
            value = (
                dot_tn(a[0][:, lanes], b[0][pl.ds(0, n)])
                + dot_tn(a[1][:, lanes], b[0][pl.ds(0, n)])
                + dot_tn(a[0][:, lanes], b[1][pl.ds(0, n)])
            )
            put(unit, value, i * 128)
            return 0

        lax.fori_loop(0, 4, part, 0)

    tall(UNITS["w2"], (hh, hl), (tabh, tabl), EDGES)
    act(PLAN[3])
    rcut = split(rsum[...])
    put(UNITS["w1c"], three(dot_tn, node_pair(), rcut))
    act(PLAN[4])
    tall(UNITS["w1b"], (sh, sl), (dph, dpl), EDGES)
    act(PLAN[5])
    load_edge.wait()

    def cut_edges(i, _):
        r = rows(i * 128, 128)
        hi, lo = split(pre[r])
        hh[r] = hi
        hl[r] = lo
        return 0

    lax.fori_loop(0, 8, cut_edges, 0)
    tall(UNITS["w1a"], (hh, hl), (dph, dpl), EDGES)
    vectors = jnp.concatenate(
        [carry[1:2], carry[0:1], nb1_grad, ngain_grad, jnp.zeros((4, W), F32)], axis=0
    )
    small = UNITS["small"] * 512
    buf[small : small + 1024] = jnp.zeros((1024, 128), F32)
    for q in range(4):
        buf[small + 8 * q : small + 8 * q + 8] = vectors[:, q * 128 : q * 128 + 128]

    def edge_out(i, _):
        r = rows(i * CH, CH)
        ecot[r] += three(dot_nt, (dph[r], dpl[r]), weight("w1a"))
        return 0

    def finish_edges():
        lax.fori_loop(0, EDGES // CH, edge_out, 0)
        stores.append(load(ecot, edge_grad_h, 13))
        ncot[...] += three(dot_nt, rcut, weight("w1c")) + three(dot_nt, dpre, weight("nw1a"))

    def collect(i, _):
        gloc[...] += two(osend_t[i], split(abuf[rows(i * 256, 256)]))
        return 0

    def finish_nodes():
        wait(abuf.at[pl.ds(0, 1016)], recv2)
        lax.fori_loop(0, 4, collect, 0)
        ncot[...] += three(dot_nt, split(gloc[...]), weight("w1b"))
        stores.append(load(ncot, node_grad_h, 14))

    act(PLAN[6])
    while due:
        step(0, 6)
    wait(sbuf.at[pl.ds(0, 1016)], send2)
    for d in started:
        d.wait_send()
    for d in stores:
        d.wait()


PLAN = (
    ("E", ),
    ("E", ),
    ("B0", ),
    ("E", "B1", ),
    ("p3", ),
    ("E", "p4", ),
    ("p5", "E", "B2", "edges", "E", "L", "E", "B3", "L", "B4", "E", "L", "B5", "E", "L", "B6", "E", "L", "B7", "E", "L", "L", "L", "nodes", ),
)


def place(*refs):
    source, target, sems = refs[:4], refs[4:15], refs[15:17]
    flat, near = refs[17], refs[18:]
    moves = []

    def move(src, mid, dst):
        n = len(moves)
        moves.append(
            (
                pltpu.make_async_copy(src, mid, sems[0].at[n]),
                pltpu.make_async_copy(mid, dst, sems[1].at[n]),
            )
        )
        moves[-1][0].start()

    first = UNITS["small"] * 512
    for i, k in enumerate((4, 6, 8, 10)):
        for q in range(4):
            r = first + 8 * q + i
            move(source[3].at[r], flat.at[r], target[k].at[pl.ds(q * 128, 128)])
    for k in range(3):
        move(source[k], near[k], target[k])
    for name, k, at in (
        ("w1a", 3, 0),
        ("w1b", 3, 512),
        ("w1c", 3, 1024),
        ("w2", 5, 0),
        ("nw1a", 7, 0),
        ("nw1b", 7, 512),
        ("nw2", 9, 0),
    ):
        for q in range(4):
            r = pl.ds((UNITS[name] + q) * 512, 512)
            move(
                source[3].at[r], flat.at[r], target[k].at[pl.ds(at, 512), pl.ds(q * 128, 128)]
            )
    for inward, outward in moves:
        inward.wait()
        outward.start()
    for inward, outward in moves:
        outward.wait()


def local(
    node_latent,
    edge_latent,
    edge_slot,
    edge_receiver,
    send_rows,
    node_cotangent,
    edge_cotangent,
    edge_w1,
    edge_b1,
    edge_w2,
    edge_gain,
    node_w1,
    node_b1,
    node_w2,
    node_gain,
):
    shape = lambda *s: jax.ShapeDtypeStruct(s, F32)
    v32 = lambda *s: pltpu.VMEM(s, F32)
    v16 = lambda *s: pltpu.VMEM(s, BF16)
    anywhere = pl.BlockSpec(memory_space=pl.ANY)
    near = pl.BlockSpec(memory_space=pltpu.VMEM)
    result = pl.pallas_call(
        kernel,
        out_shape=(
            shape(NODES, W),
            shape(NODES, W),
            shape(EDGES, W),
            shape(FLAT, 128),
        ),
        in_specs=[near] * 3 + [anywhere] * 12,
        out_specs=[anywhere] * 4,
        scratch_shapes=[
            v32(4, W),
            v32(NODES, W),
            v16(NODES, W),
            v16(NODES, W),
            v32(NODES, W),
            v32(EDGES, W),
            v32(EDGES, W),
            v16(3584, W),
            v16(3584, W),
            v32(EDGES, W),
            v32(EDGES, W),
            v32(EDGES, W),
            v16(EDGES, SLOTS),
            v16(EDGES, NODES),
            v16(4, NODES, 256),
            v16(EDGES, NODES),
            v16(4, NODES, 256),
            v16(SLOTS, W),
            v16(SLOTS, W),
            v16(EDGES, W),
            v16(EDGES, W),
            v16(EDGES, W),
            v16(EDGES, W),
            v16(EDGES, W),
            v16(EDGES, W),
            v32(EDGES, 128),
            v32(NODES, W),
            v32(NODES, W),
            v32(8, W),
            v32(NODES, W),
            v32(NODES, W),
            v32(FLAT, 128),
            v32(FLAT, 128),
            v32(7560, 128),
            pltpu.SemaphoreType.DMA((32,)),
            pltpu.SemaphoreType.DMA,
            pltpu.SemaphoreType.DMA,
            pltpu.SemaphoreType.DMA,
            pltpu.SemaphoreType.DMA,
            pltpu.SemaphoreType.DMA((6, SEMS)),
            pltpu.SemaphoreType.DMA((6, SEMS)),
        ],
        compiler_params=pltpu.CompilerParams(
            collective_id=1, has_side_effects=True, vmem_limit_bytes=63 << 20
        ),
    )(
        edge_slot.reshape(8, 128),
        edge_receiver.reshape(8, 128),
        send_rows.reshape(8, 128),
        edge_b1,
        edge_gain,
        node_b1,
        node_gain,
        node_latent,
        edge_latent,
        node_cotangent,
        edge_cotangent,
        edge_w1,
        edge_w2,
        node_w1,
        node_w2,
    )
    return pl.pallas_call(
        place,
        out_shape=(
            shape(NODES, W),
            shape(NODES, W),
            shape(EDGES, W),
            shape(1536, W),
            shape(512),
            shape(512, W),
            shape(512),
            shape(1024, W),
            shape(512),
            shape(512, W),
            shape(512),
        ),
        in_specs=[anywhere] * 4,
        out_specs=(anywhere,) * 11,
        scratch_shapes=[
            pltpu.SemaphoreType.DMA((47,)),
            pltpu.SemaphoreType.DMA((47,)),
            v32(FLAT, 128),
            v32(NODES, W),
            v32(NODES, W),
            v32(EDGES, W),
        ],
        compiler_params=pltpu.CompilerParams(vmem_limit_bytes=60 << 20),
    )(*result)


def solution(mesh):
    return jax.shard_map(
        local,
        mesh=mesh,
        in_specs=(
            P(("wide", "narrow"), None),
            P(("wide", "narrow"), None),
            P(("wide", "narrow")),
            P(("wide", "narrow")),
            P(("wide", "narrow"), None, None),
            P(("wide", "narrow"), None),
            P(("wide", "narrow"), None),
            P(),
            P(),
            P(),
            P(),
            P(),
            P(),
            P(),
            P(),
        ),
        out_specs=(
            P(("wide", "narrow"), None),
            P(("wide", "narrow"), None),
            P(("wide", "narrow"), None),
            P(),
            P(),
            P(),
            P(),
            P(),
            P(),
            P(),
            P(),
        ),
        check_vma=False,
    )
```

```python
import functools

import jax
import jax.numpy as jnp
from jax import lax
from jax.experimental import pallas as pl
from jax.experimental.pallas import tpu as pltpu
from jax.sharding import PartitionSpec as P

MESH = pl.DeviceIdType.MESH
F32, BF16, I32 = jnp.float32, jnp.bfloat16, jnp.int32
W = 512
NODES = 256
EDGES = 1024
SLOTS = 1280
CH = 256

FLAT = 15360
ORDERS = ((0, 1, 2), (1, 2, 0), (2, 0, 1))
SEMS = 30
PARTS = (
    (0, 0, 16, 0),
    (1, 2048, 16, 1008),
    (2, 4096, 16, 2016),
    (0, 6144, 24, 3024),
    (1, 9216, 24, 4536),
    (2, 12288, 24, 6048),
)
UNITS = {"nw2": 0, "nw1a": 4, "nw1b": 8, "w2": 12, "w1c": 16, "w1b": 20, "w1a": 24, "small": 28}
WROW = {"w1a": 0, "w1b": 512, "w1c": 1024, "w2": 1536, "nw1a": 2048, "nw1b": 2560, "nw2": 3072}


def coords():
    w = lax.axis_index("wide")
    n = lax.axis_index("narrow")
    return w % 4, n // 2, w // 4, n % 2


def device(x, y, z, c):
    return (z * 4 + x, y * 2 + c)


def wait(ref, sem):
    pltpu.make_async_copy(ref, ref, sem).wait()


def rows(start, n):
    return pl.ds(pl.multiple_of(start, 8), n)


def split(v):
    high = v.astype(BF16)
    return high, (v - high.astype(F32)).astype(BF16)


def dot(a, b):
    return jnp.dot(a, b, preferred_element_type=F32)


def dot_nt(a, b):
    return lax.dot_general(a, b, (((1,), (1,)), ((), ())), preferred_element_type=F32)


def dot_tn(a, b):
    return lax.dot_general(a, b, (((0,), (0,)), ((), ())), preferred_element_type=F32)


def three(op, a, b):
    ka = 0 if op is dot_tn else 1
    kb = 1 if op is dot_nt else 0
    return op(jnp.concatenate([a[0], a[1], a[0]], axis=ka), jnp.concatenate([b[0], b[0], b[1]], axis=kb))


def two(one_hot, pair):
    return dot(
        jnp.concatenate([one_hot, one_hot], axis=1), jnp.concatenate([pair[0], pair[1]], axis=0)
    )


def reduce_part(part, buf, out, halves_in, send, recv, started):
    rot, base, leaf, into = PARTS[part]
    here = coords()
    core = here[3]
    order = ORDERS[rot]
    pos = [here[a] for a in order]
    sizes = (16 * leaf, 4 * leaf, leaf)

    def shifted(stage, by):
        c = list(here)
        c[order[stage]] = (c[order[stage]] + by) % 4
        return device(*c)

    sibling = device(here[0], here[1], here[2], 1 - core)

    def post(src, dst, k, to):
        d = pltpu.make_async_remote_copy(
            src_ref=src,
            dst_ref=dst,
            send_sem=send.at[part, k],
            recv_sem=recv.at[part, k],
            device_id=to,
            device_id_type=MESH,
        )
        d.start()
        started.append(d)

    mine = base + core * 64 * leaf
    other = base + (1 - core) * 64 * leaf
    L = sizes[0]
    A = L // 2
    j = pos[0]
    spot = lambda q: mine + ((j + q) % 4) * L
    for m, q in enumerate((2, -1, 1, 0)):
        r = rows(other + ((j + q) % 4) * L, L)
        post(buf.at[r], out.at[r], m, sibling)
    yield

    def core_add(m, q):
        wait(out.at[rows(spot(q), L)], recv.at[part, m])

        def add(i, _):
            r = rows(spot(q) + i * A, A)
            buf[r] = buf[r] + out[r]
            return 0

        lax.fori_loop(0, 2, add, 0)

    up, down = shifted(0, 1), shifted(0, -1)
    first_a, first_b = rows(into, A), rows(into + A, A)
    plus_a, plus_b = rows(into + L, A), rows(into + L + A, A)
    minus_a, minus_b = rows(into + 2 * L, A), rows(into + 2 * L + A, A)
    land = lambda r: halves_in.at[r]
    core_add(0, 2)
    post(buf.at[rows(spot(2), A)], land(first_a), 4, down)
    post(buf.at[rows(spot(2) + A, A)], land(first_b), 5, up)
    core_add(1, -1)
    post(buf.at[rows(spot(-1) + A, A)], land(plus_b), 6, down)
    core_add(2, 1)
    post(buf.at[rows(spot(1), A)], land(minus_a), 7, up)
    yield
    wait(land(first_a), recv.at[part, 4])
    r = rows(spot(-1), A)
    buf[r] = buf[r] + halves_in[first_a]
    post(buf.at[r], land(plus_a), 8, down)
    wait(land(first_b), recv.at[part, 5])
    r = rows(spot(1) + A, A)
    buf[r] = buf[r] + halves_in[first_b]
    post(buf.at[r], land(minus_b), 9, up)
    yield
    core_add(3, 0)
    wait(land(plus_b), recv.at[part, 6])
    wait(land(minus_a), recv.at[part, 7])
    wait(land(plus_a), recv.at[part, 8])
    wait(land(minus_b), recv.at[part, 9])
    r = rows(spot(0), L)
    buf[r] = buf[r] + halves_in[rows(into + L, L)] + halves_in[rows(into + 2 * L, L)]
    region = mine + j * L
    into += 3 * L
    for s in (1, 2):
        L = sizes[s]
        j = pos[s]
        k = 10 + 3 * (s - 1)
        for m, q in enumerate((2, 1, 3)):
            post(
                buf.at[rows(region + ((j + q) % 4) * L, L)],
                land(rows(into + m * L, L)),
                k + m,
                shifted(s, q),
            )
        yield
        for m in range(3):
            wait(land(rows(into + m * L, L)), recv.at[part, k + m])
        r = rows(region + j * L, L)
        total = buf[r] + halves_in[rows(into, L)]
        total = total + halves_in[rows(into + L, L)] + halves_in[rows(into + 2 * L, L)]
        if s == 1:
            buf[r] = total
        else:
            out[r] = total
        region = region + j * L
        into += 3 * L
    for s in (2, 1):
        L = sizes[s]
        j = pos[s]
        k = 16 + 3 * (2 - s)
        own = out.at[rows(region, L)]
        for m, q in enumerate((2, 1, 3)):
            post(own, own, k + m, shifted(s, q))
        yield
        region = region - j * L
        for m, q in enumerate((2, 3, 1)):
            wait(out.at[rows(region + ((j + q) % 4) * L, L)], recv.at[part, k + m])
    L = sizes[0]
    j = pos[0]
    own = out.at[rows(spot(0), L)]
    post(own, own, 22, up)
    post(own, own, 23, down)
    post(own, own, 26, sibling)
    yield
    left, right = out.at[rows(spot(-1), L)], out.at[rows(spot(1), L)]
    wait(left, recv.at[part, 22])
    piece = out.at[rows(spot(-1), A)]
    post(piece, piece, 24, up)
    post(left, left, 27, sibling)
    wait(right, recv.at[part, 23])
    piece = out.at[rows(spot(1) + A, A)]
    post(piece, piece, 25, down)
    post(right, right, 28, sibling)
    yield
    wait(out.at[rows(spot(2), A)], recv.at[part, 24])
    wait(out.at[rows(spot(2) + A, A)], recv.at[part, 25])
    opposite = out.at[rows(spot(2), L)]
    post(opposite, opposite, 29, sibling)
    yield
    for n in range(4):
        wait(out.at[rows(other, L)], recv.at[part, 26 + n])


def kernel(
    slot_ref, receiver_ref, list_ref, eb1_h, eg_h, nb1_h, ng_h,
    node_h, edge_h, ncot_h, ecot_h, w1_h, w2_h, nw1_h, nw2_h,
    new_nodes_h, node_grad_h, edge_grad_h, flat_h,
    vector_ref, node_v, node_hi, node_lo, ncot, ecot, pre, whi, wlo, sbuf, rbuf, abuf,
    oslot, orecv, orecv_t, osend, osend_t, tabh, tabl, sh, sl, hh, hl, dph, dpl,
    rstd_v, agg, npre, carry, gloc, rsum, buf, out, halves_in,
    lsem, send1, recv1, send2, recv2, send, recv,
):
    x, y, z, c = coords()
    me = (z * 4 + x) * 8 + y * 2 + c

    def peer(d):
        return (z + d // 32) % 4 * 4 + (x + d // 8) % 4, (y + d // 2) % 4 * 2 + (c + d) % 2

    def load(src, dst, k):
        d = pltpu.make_async_copy(src, dst, lsem.at[k])
        d.start()
        return d

    xhat = rbuf
    load_node = load(node_h, node_v, 0)
    load_vectors = [
        load(ref, vector_ref.at[i], 21 + i) for i, ref in enumerate((eb1_h, eg_h, nb1_h, ng_h))
    ]
    load_edge = load(edge_h, pre, 1)
    load_ncot = load(ncot_h, ncot, 2)
    blocks = [(w1_h, 0), (w1_h, 512), (w1_h, 1024), (w2_h, 0), (nw1_h, 0), (nw1_h, 512), (nw2_h, 0)]

    def load_weights(b):
        src, at = blocks[b]
        return load(src.at[pl.ds(at, 512)], ecot.at[pl.ds(b % 2 * 512, 512)], 3 + b)

    loading = {b: load_weights(b) for b in (0, 1)}
    barrier = pltpu.get_barrier_semaphore()

    def greet(i, _):
        for q in range(8):
            pl.semaphore_signal(barrier, inc=1, device_id=peer(i * 8 + q), device_id_type=MESH)
        return 0

    for i in range(1, 8):
        pl.semaphore_signal(barrier, inc=1, device_id=peer(i), device_id_type=MESH)
    lax.fori_loop(1, 16, greet, 0)

    def line(ref, i):
        return jnp.broadcast_to(ref[pl.ds(i, 1), :], (128, 128))

    def across(i, ref, store, n):
        lanes = lax.broadcasted_iota(I32, (128, 128), 1)
        column = line(ref, i).T
        for q in range(n // 128):
            store[rows(i * 128, 128), q * 128 : q * 128 + 128] = jnp.where(
                column == lanes + q * 128, 1.0, 0.0
            ).astype(BF16)

    def hot(i, _):
        across(i, list_ref, osend, NODES)
        return 0

    lax.fori_loop(0, 8, hot, 0)
    load_node.wait()
    for d in load_vectors:
        d.wait()
    nhi, nlo = split(node_v[...])
    node_hi[...] = nhi
    node_lo[...] = nlo

    def gather(i, _):
        r = rows(i * CH, CH)
        sbuf[r] = two(osend[r], (node_hi[...], node_lo[...]))
        return 0

    lax.fori_loop(0, EDGES // CH, gather, 0)
    mine8 = rows(me * 8, 8)
    rbuf[mine8] = sbuf[mine8]
    pl.semaphore_wait(barrier, 127)

    def send_rows(i, _):
        w, n = peer(i * 37 % 128)
        pltpu.make_async_remote_copy(
            src_ref=sbuf.at[rows((w * 8 + n) * 8, 8)],
            dst_ref=rbuf.at[mine8],
            send_sem=send1,
            recv_sem=recv1,
            device_id=(w, n),
            device_id_type=MESH,
        ).start()
        return 0

    lax.fori_loop(1, 128, send_rows, 0)

    for b in range(7):
        loading[b].wait()

        def cut(i, _, b=b):
            hi, lo = split(ecot[rows(b % 2 * 512 + i * 128, 128)])
            whi[rows(b * 512 + i * 128, 128)] = hi
            wlo[rows(b * 512 + i * 128, 128)] = lo
            return 0

        lax.fori_loop(0, 4, cut, 0)
        if b + 2 < 7:
            loading[b + 2] = load_weights(b + 2)
    load_ecot = load(ecot_h, ecot, 10)

    def weight(name):
        r = pl.ds(WROW[name], 512)
        return whi[r], wlo[r]

    def hot_edges(i, _):
        across(i, slot_ref, oslot, SLOTS)
        across(i, receiver_ref, orecv, NODES)
        return 0

    lax.fori_loop(0, 8, hot_edges, 0)

    def down(ref, i, first, n):
        return jnp.where(
            jnp.broadcast_to(ref[pl.ds(i, 1), :], (n, 128))
            == lax.broadcasted_iota(I32, (n, 128), 0) + first,
            1.0,
            0.0,
        ).astype(BF16)

    for i in range(8):
        lanes = slice(i % 2 * 128, i % 2 * 128 + 128)
        orecv_t[i // 2, :, lanes] = down(receiver_ref, i, 0, NODES)
        osend_t[i // 2, :, lanes] = down(list_ref, i, 0, NODES)

    node_pair = lambda: (node_hi[...], node_lo[...])
    projected = split(three(dot, node_pair(), weight("w1c")))
    agg[...] = projected[0].astype(F32)
    gloc[...] = projected[1].astype(F32)
    npre[...] = three(dot, node_pair(), weight("nw1a")) + vector_ref[2:3, :]
    load_edge.wait()

    def first_layer(i, _):
        r = rows(i * CH, CH)
        pair = split(pre[r])
        pre[r] = (
            three(dot, pair, weight("w1a"))
            + two(orecv[r], (agg[...].astype(BF16), gloc[...].astype(BF16)))
            + vector_ref[0:1, :]
        )
        return 0

    lax.fori_loop(0, EDGES // CH, first_layer, 0)
    tabh[0:NODES] = node_hi[...]
    tabl[0:NODES] = node_lo[...]
    agg[...] = jnp.zeros_like(agg)

    wait(rbuf.at[pl.ds(0, 1016)], recv1)
    wait(sbuf.at[pl.ds(0, 1016)], send1)

    def cut_table(i, _):
        hi, lo = split(rbuf[rows(i * 256, 256)])
        tabh[rows(256 + i * 256, 256)] = hi
        tabl[rows(256 + i * 256, 256)] = lo
        return 0

    lax.fori_loop(0, 4, cut_table, 0)

    def forward(i, _):
        r = rows(i * 512, 512)
        hot = oslot[r, 0:SLOTS]
        senders = dot(hot, tabh[...]).astype(BF16), dot(hot, tabl[...]).astype(BF16)
        sh[r] = senders[0]
        sl[r] = senders[1]
        v = pre[r] + three(dot, senders, weight("w1b"))
        s = 1.0 / (1.0 + jnp.exp(-v))
        pre[r] = s * (1.0 + v * (1.0 - s))
        hidden = split(v * s)
        hh[r] = hidden[0]
        hl[r] = hidden[1]
        zed = three(dot, hidden, weight("w2"))
        centre = zed - jnp.mean(zed, axis=1, keepdims=True)
        rstd = lax.rsqrt(jnp.mean(centre * centre, axis=1, keepdims=True) + 1e-05)
        scaled = centre * rstd
        xhat[r] = scaled
        rstd_v[r] = jnp.broadcast_to(rstd, (512, 128))
        pair = split(scaled)
        agg[...] += two(orecv_t[2 * i], (pair[0][:256], pair[1][:256]))
        agg[...] += two(orecv_t[2 * i + 1], (pair[0][256:], pair[1][256:]))
        return 0

    lax.fori_loop(0, 2, forward, 0)

    aggregate = split(agg[...] * vector_ref[1:2, :])
    v = npre[...] + three(dot, aggregate, weight("nw1b"))
    s = 1.0 / (1.0 + jnp.exp(-v))
    slope = s * (1.0 + v * (1.0 - s))
    hidden = split(v * s)
    zed = three(dot, hidden, weight("nw2"))
    centre = zed - jnp.mean(zed, axis=1, keepdims=True)
    rstd = lax.rsqrt(jnp.mean(centre * centre, axis=1, keepdims=True) + 1e-05)
    scaled = centre * rstd
    npre[...] = node_v[...] + scaled * vector_ref[3:4, :]
    store_nodes = load(npre, new_nodes_h, 11)
    load_ncot.wait()
    ngain_grad = jnp.sum(ncot[...] * scaled, axis=0, keepdims=True)
    cot = ncot[...] * vector_ref[3:4, :]
    dz = split(
        rstd
        * (
            cot
            - jnp.mean(cot, axis=1, keepdims=True)
            - scaled * jnp.mean(cot * scaled, axis=1, keepdims=True)
        )
    )
    dpre = three(dot_nt, dz, weight("nw2")) * slope
    nb1_grad = jnp.sum(dpre, axis=0, keepdims=True)
    dpre = split(dpre)
    dagg = split(three(dot_nt, dpre, weight("nw1b")))

    def put(unit, value, first=0):
        for q in range(4):
            buf[rows((unit + q) * 512 + first, value.shape[0])] = value[:, q * 128 : q * 128 + 128]

    put(UNITS["nw2"], three(dot_tn, hidden, dz))
    put(UNITS["nw1a"], three(dot_tn, node_pair(), dpre))
    put(UNITS["nw1b"], three(dot_tn, aggregate, dpre))
    started = []
    parts = [reduce_part(p, buf, out, halves_in, send, recv, started) for p in range(6)]
    stores = [store_nodes]
    due = list(range(6))

    def step(first, last):
        for p in range(first, last):
            if p in due and next(parts[p], 0) == 0:
                due.remove(p)
                r = pl.ds(PARTS[p][1], 128 * PARTS[p][2])
                stores.append(load(out.at[r], flat_h.at[r], 15 + p))

    def act(tokens):
        for t in tokens:
            if t == "E":
                step(0, 3)
            elif t == "L":
                step(3, 6)
            elif t[0] == "p":
                step(int(t[1]), int(t[1]) + 1)
            elif t[0] == "B":
                n = int(t[1])
                give(max(1, 16 * n), 16 * n + 16)
            elif t == "edges":
                finish_edges()
            else:
                finish_nodes()

    act(PLAN[0])

    load_ecot.wait()
    carry[...] = jnp.zeros_like(carry)
    agg[...] = dagg[0].astype(F32)
    gloc[...] = dagg[1].astype(F32)

    def backward(i, _):
        r = rows(i * 512, 512)
        scaled = xhat[r]
        mcot = ecot[r] + two(orecv[r], (agg[...].astype(BF16), gloc[...].astype(BF16)))
        carry[0:1] += jnp.sum(mcot * scaled, axis=0, keepdims=True)
        cot = mcot * vector_ref[1:2, :]
        dz = split(
            rstd_v[r][:, 0:1]
            * (
                cot
                - jnp.mean(cot, axis=1, keepdims=True)
                - scaled * jnp.mean(cot * scaled, axis=1, keepdims=True)
            )
        )
        tabh[r] = dz[0]
        tabl[r] = dz[1]
        dpre = three(dot_nt, dz, weight("w2")) * pre[r]
        carry[1:2] += jnp.sum(dpre, axis=0, keepdims=True)
        dpre = split(dpre)
        dph[r] = dpre[0]
        dpl[r] = dpre[1]
        return 0

    lax.fori_loop(0, 2, backward, 0)
    act(PLAN[1])
    load_edge = load(edge_h, pre, 12)

    def scatter(first):
        for i in range(8):
            oslot[0:256, i * 128 : i * 128 + 128] = down(slot_ref, i, first, 256)
        return two(oslot[0:256, 0:EDGES], (dph[...], dpl[...]))

    def plane(n, _):
        at = (z + n) % 4 * 256
        sbuf[rows(at, 256)] = scatter(NODES + at)
        return 0

    def give(first, last):
        def one(i, _):
            w, nn = peer(i * 37 % 128)
            pltpu.make_async_remote_copy(
                src_ref=sbuf.at[rows((w * 8 + nn) * 8, 8)],
                dst_ref=abuf.at[mine8],
                send_sem=send2,
                recv_sem=recv2,
                device_id=(w, nn),
                device_id_type=MESH,
            ).start()
            return 0

        lax.fori_loop(first, last, one, 0)

    lax.fori_loop(0, 4, plane, 0)
    act(PLAN[2])
    abuf[mine8] = sbuf[mine8]
    gloc[...] = scatter(0)
    rsum[...] = sum(
        two(orecv_t[i], (dph[pl.ds(i * CH, CH)], dpl[pl.ds(i * CH, CH)])) for i in range(4)
    )

    def tall(unit, a, b, n):
        def part(i, _):
            lanes = pl.ds(pl.multiple_of(i * 128, 128), 128)
            value = three(
                dot_tn, (a[0][:, lanes], a[1][:, lanes]), (b[0][pl.ds(0, n)], b[1][pl.ds(0, n)])
            )
            put(unit, value, i * 128)
            return 0

        lax.fori_loop(0, 4, part, 0)

    tall(UNITS["w2"], (hh, hl), (tabh, tabl), EDGES)
    act(PLAN[3])
    rcut = split(rsum[...])
    put(UNITS["w1c"], three(dot_tn, node_pair(), rcut))
    act(PLAN[4])
    tall(UNITS["w1b"], (sh, sl), (dph, dpl), EDGES)
    act(PLAN[5])
    load_edge.wait()

    def cut_edges(i, _):
        r = rows(i * 128, 128)
        hi, lo = split(pre[r])
        hh[r] = hi
        hl[r] = lo
        return 0

    lax.fori_loop(0, 8, cut_edges, 0)
    tall(UNITS["w1a"], (hh, hl), (dph, dpl), EDGES)
    vectors = jnp.concatenate(
        [carry[1:2], carry[0:1], nb1_grad, ngain_grad, jnp.zeros((4, W), F32)], axis=0
    )
    small = UNITS["small"] * 512
    buf[small : small + 1024] = jnp.zeros((1024, 128), F32)
    for q in range(4):
        buf[small + 8 * q : small + 8 * q + 8] = vectors[:, q * 128 : q * 128 + 128]

    def edge_out(i, _):
        r = rows(i * CH, CH)
        ecot[r] += three(dot_nt, (dph[r], dpl[r]), weight("w1a"))
        return 0

    def finish_edges():
        lax.fori_loop(0, EDGES // CH, edge_out, 0)
        stores.append(load(ecot, edge_grad_h, 13))
        ncot[...] += three(dot_nt, rcut, weight("w1c")) + three(dot_nt, dpre, weight("nw1a"))

    def collect(i, _):
        gloc[...] += two(osend_t[i], split(abuf[rows(i * 256, 256)]))
        return 0

    def finish_nodes():
        wait(abuf.at[pl.ds(0, 1016)], recv2)
        lax.fori_loop(0, 4, collect, 0)
        ncot[...] += three(dot_nt, split(gloc[...]), weight("w1b"))
        stores.append(load(ncot, node_grad_h, 14))

    act(PLAN[6])
    while due:
        step(0, 6)
    wait(sbuf.at[pl.ds(0, 1016)], send2)
    for d in started:
        d.wait_send()
    for d in stores:
        d.wait()


PLAN = (
    ("E", ),
    ("E", ),
    ("B0", ),
    ("E", "B1", ),
    ("p3", ),
    ("E", "p4", ),
    ("p5", "E", "B2", "edges", "L", "E", "L", "E", "B3", "L", "E", "B4", "L", "E", "B5", "L", "E", "B6", "L", "E", "B7", "L", "L", "nodes", ),
)


def place(*refs):
    source, target, sems = refs[:4], refs[4:15], refs[15:17]
    flat, near = refs[17], refs[18:]
    moves = []

    def move(src, mid, dst):
        n = len(moves)
        moves.append(
            (
                pltpu.make_async_copy(src, mid, sems[0].at[n]),
                pltpu.make_async_copy(mid, dst, sems[1].at[n]),
            )
        )
        moves[-1][0].start()

    first = UNITS["small"] * 512
    for i, k in enumerate((4, 6, 8, 10)):
        for q in range(4):
            r = first + 8 * q + i
            move(source[3].at[r], flat.at[r], target[k].at[pl.ds(q * 128, 128)])
    for k in range(3):
        move(source[k], near[k], target[k])
    for name, k, at in (
        ("w1a", 3, 0),
        ("w1b", 3, 512),
        ("w1c", 3, 1024),
        ("w2", 5, 0),
        ("nw1a", 7, 0),
        ("nw1b", 7, 512),
        ("nw2", 9, 0),
    ):
        for q in range(4):
            r = pl.ds((UNITS[name] + q) * 512, 512)
            move(
                source[3].at[r], flat.at[r], target[k].at[pl.ds(at, 512), pl.ds(q * 128, 128)]
            )
    for inward, outward in moves:
        inward.wait()
        outward.start()
    for inward, outward in moves:
        outward.wait()


def local(
    node_latent,
    edge_latent,
    edge_slot,
    edge_receiver,
    send_rows,
    node_cotangent,
    edge_cotangent,
    edge_w1,
    edge_b1,
    edge_w2,
    edge_gain,
    node_w1,
    node_b1,
    node_w2,
    node_gain,
):
    shape = lambda *s: jax.ShapeDtypeStruct(s, F32)
    v32 = lambda *s: pltpu.VMEM(s, F32)
    v16 = lambda *s: pltpu.VMEM(s, BF16)
    anywhere = pl.BlockSpec(memory_space=pl.ANY)
    near = pl.BlockSpec(memory_space=pltpu.VMEM)
    result = pl.pallas_call(
        kernel,
        out_shape=(
            shape(NODES, W),
            shape(NODES, W),
            shape(EDGES, W),
            shape(FLAT, 128),
        ),
        in_specs=[near] * 3 + [anywhere] * 12,
        out_specs=[anywhere] * 4,
        scratch_shapes=[
            v32(4, W),
            v32(NODES, W),
            v16(NODES, W),
            v16(NODES, W),
            v32(NODES, W),
            v32(EDGES, W),
            v32(EDGES, W),
            v16(3584, W),
            v16(3584, W),
            v32(EDGES, W),
            v32(EDGES, W),
            v32(EDGES, W),
            v16(EDGES, SLOTS),
            v16(EDGES, NODES),
            v16(4, NODES, 256),
            v16(EDGES, NODES),
            v16(4, NODES, 256),
            v16(SLOTS, W),
            v16(SLOTS, W),
            v16(EDGES, W),
            v16(EDGES, W),
            v16(EDGES, W),
            v16(EDGES, W),
            v16(EDGES, W),
            v16(EDGES, W),
            v32(EDGES, 128),
            v32(NODES, W),
            v32(NODES, W),
            v32(8, W),
            v32(NODES, W),
            v32(NODES, W),
            v32(FLAT, 128),
            v32(FLAT, 128),
            v32(7560, 128),
            pltpu.SemaphoreType.DMA((32,)),
            pltpu.SemaphoreType.DMA,
            pltpu.SemaphoreType.DMA,
            pltpu.SemaphoreType.DMA,
            pltpu.SemaphoreType.DMA,
            pltpu.SemaphoreType.DMA((6, SEMS)),
            pltpu.SemaphoreType.DMA((6, SEMS)),
        ],
        compiler_params=pltpu.CompilerParams(
            collective_id=1, has_side_effects=True, vmem_limit_bytes=63 << 20
        ),
    )(
        edge_slot.reshape(8, 128),
        edge_receiver.reshape(8, 128),
        send_rows.reshape(8, 128),
        edge_b1,
        edge_gain,
        node_b1,
        node_gain,
        node_latent,
        edge_latent,
        node_cotangent,
        edge_cotangent,
        edge_w1,
        edge_w2,
        node_w1,
        node_w2,
    )
    return pl.pallas_call(
        place,
        out_shape=(
            shape(NODES, W),
            shape(NODES, W),
            shape(EDGES, W),
            shape(1536, W),
            shape(512),
            shape(512, W),
            shape(512),
            shape(1024, W),
            shape(512),
            shape(512, W),
            shape(512),
        ),
        in_specs=[anywhere] * 4,
        out_specs=(anywhere,) * 11,
        scratch_shapes=[
            pltpu.SemaphoreType.DMA((47,)),
            pltpu.SemaphoreType.DMA((47,)),
            v32(FLAT, 128),
            v32(NODES, W),
            v32(NODES, W),
            v32(EDGES, W),
        ],
        compiler_params=pltpu.CompilerParams(vmem_limit_bytes=60 << 20),
    )(*result)


def solution(mesh):
    return jax.shard_map(
        local,
        mesh=mesh,
        in_specs=(
            P(("wide", "narrow"), None),
            P(("wide", "narrow"), None),
            P(("wide", "narrow")),
            P(("wide", "narrow")),
            P(("wide", "narrow"), None, None),
            P(("wide", "narrow"), None),
            P(("wide", "narrow"), None),
            P(),
            P(),
            P(),
            P(),
            P(),
            P(),
            P(),
            P(),
        ),
        out_specs=(
            P(("wide", "narrow"), None),
            P(("wide", "narrow"), None),
            P(("wide", "narrow"), None),
            P(),
            P(),
            P(),
            P(),
            P(),
            P(),
            P(),
            P(),
        ),
        check_vma=False,
    )
```
